32 devices in a mesh: req: 8 (over y, x, core), head: 4 (over z).
Axes of the slice: x: 2, y: 2, z: 4, core: 2. Of those that a mesh axis runs over, the one named last changes fastest.
Arguments:
- hidden_in: bfloat16 [2048, 4096], P('req', 'head'), may hold values from -6 to 6
- norm_gain: float32 [4096], replicated, may hold values from 0.25 to 1.75
- norm_shift: float32 [4096], replicated, may hold values from -3 to 3
- attend_weight: bfloat16 [4096, 3, 2048], P(None, None, 'head'), may hold values from -0.09375 to 0.09375
- output_weight: bfloat16 [2048, 4096], P('head'), may hold values from -0.125 to 0.125
- up_weight: bfloat16 [4096, 8192], P('req', 'head'), may hold values from -0.09375 to 0.09375
- up_bias: float32 [8192], P('head'), may hold values from -3 to 3
- down_weight: bfloat16 [8192, 4096], P('head', 'req'), may hold values from -0.0625 to 0.0625
- down_bias: float32 [4096], P('head'), may hold values from -3 to 3
- key_cache: bfloat16 [16, 1536, 2048], P('req', None, 'head'), may hold values from -160 to 160
- value_cache: bfloat16 [16, 1536, 2048], P('req', None, 'head'), may hold values from -5 to 5
- cached_len: int32 [16], P('req'), may hold values from 1 to 1536, as said below
Outputs:
- hidden_out: bfloat16 [2048, 4096], P('req', 'head')
- new_keys: bfloat16 [16, 128, 2048], P('req', None, 'head')
- new_values: bfloat16 [16, 128, 2048], P('req', None, 'head')
The draws below stay inside these ranges and needn't reach their ends.
Inputs may be any that keep to these rules, and one draw needn't show every extreme that they name: `cached_len`: each cached length is under 64 or between 768 and 1536; some request has exactly 1536.
All inputs are finite; a program needn't handle non-finite values.
Results may differ from the reference program's by a relative error of at most 0.012.
Values may be sent and summed in bfloat16 or wider, within the bound.
No kernel may reach another device: no remote copies, remote signals or barrier semaphores. Data moves between devices by JAX's collectives and lax.ppermute only.
A program may use at most 128 MiB of HBM per device.

```python
import jax
import jax.numpy as jnp
from jax import lax

D = 4096
HD = 256
HEADS = 8
ROT = 64
FF = 8192
GROUP = 128
CMAX = 1536
SHORT = 64
REQS = 16
TOKENS = 2048


def draw_key_cache(key, part):
    first_key = jax.random.fold_in(jax.random.fold_in(key, 11), 0)
    base = jnp.clip(jax.random.normal(first_key, (REQS, CMAX, HEADS * HD), jnp.float32), -4.0, 4.0)
    return base.astype(jnp.bfloat16)


def draw_cached_len(key, part):
    coin_key, short_key, long_key, pick_key = jax.random.split(jax.random.fold_in(key, 23), 4)
    coins = jax.random.randint(coin_key, (REQS,), 0, 2)
    short_len = jax.random.randint(short_key, (REQS,), 1, SHORT)
    long_len = jax.random.randint(long_key, (REQS,), CMAX // 2, CMAX + 1)
    lengths = jnp.where(coins == 1, long_len, short_len)
    chosen = jax.random.randint(pick_key, (), 0, REQS)
    lengths = jnp.where(jnp.arange(REQS) == chosen, CMAX, lengths)
    return lengths.astype(jnp.int32)


def level_of(key, extent, cuts, low, top_value):
    factor_of, own = 1.0, jax.random.fold_in(key, 6)
    for dim, parts in cuts:
        draws = jnp.exp(jax.random.uniform(jax.random.fold_in(own, dim), (parts,), jnp.float32, low / len(cuts), top_value / len(cuts)))
        factor_of = factor_of * jnp.repeat(draws, extent[dim] // parts).reshape([-1 if axis == dim else 1 for axis in range(len(extent))])
    return factor_of


def gaussian(key, dims, deviation, most, cuts=(), held_as=jnp.bfloat16):
    loudness = level_of(key, dims, cuts, -0.22, 0.18) if cuts else 1.0
    drawn = jax.random.normal(key, dims, jnp.float32) * deviation * loudness
    return jnp.minimum(jnp.maximum(drawn, -most), most).astype(held_as)


def setup_inputs(seed: int = 0) -> dict:
    keys = jax.random.split(jax.random.key(seed), 13)
    return {
        "hidden_in": gaussian(keys[0], (TOKENS, D), 1.0, 6.0, ((0, 8), (1, 4))),
        "norm_gain": jnp.clip(1.0 + 0.15 * jax.random.normal(keys[1], (D,), jnp.float32), 0.25, 1.75),
        "norm_shift": gaussian(keys[2], (D,), 0.5, 3.0, (), jnp.float32),
        "attend_weight": gaussian(keys[3], (D, 3, HEADS * HD), D ** -0.5, 0.09375, ((2, 4),)),
        "output_weight": gaussian(keys[4], (HEADS * HD, D), (HEADS * HD) ** -0.5, 0.125, ((0, 4),)),
        "up_weight": gaussian(keys[5], (D, FF), D ** -0.5, 0.09375, ((0, 8), (1, 4))),
        "up_bias": gaussian(keys[6], (FF,), 0.5, 3.0, ((0, 4),), jnp.float32),
        "down_weight": gaussian(keys[7], (FF, D), FF ** -0.5, 0.0625, ((0, 4), (1, 8))),
        "down_bias": gaussian(keys[8], (D,), 0.5, 3.0, ((0, 4),), jnp.float32),
        "key_cache": draw_key_cache(jax.random.fold_in(keys[12], 71), 0),
        "value_cache": gaussian(keys[10], (REQS, CMAX, HEADS * HD), 1.0, 5.0, ((0, 8), (2, 4))),
        "cached_len": draw_cached_len(jax.random.fold_in(keys[12], 71), 0),
    }


epsilon = 1e-05

def layer_norm(values, gain_vec, shift_vec):
    floats = values.astype(jnp.float32)
    center = floats - lax.optimization_barrier(jnp.mean(floats, axis=-1, keepdims=True))
    spread = lax.optimization_barrier(jnp.mean(center * center, axis=-1, keepdims=True))
    return center * lax.rsqrt(spread + epsilon) * gain_vec + shift_vec

def rotate_pairs(tensor, positions):
    halves = ROT // 2
    frequency = 10000.0 ** (-(jnp.arange(halves, dtype=jnp.float32) * 2.0) / ROT)
    angles = positions.astype(jnp.float32)[:, :, None] * frequency
    cosine = jnp.cos(angles)[:, :, None, :]
    sine_part = jnp.sin(angles)[:, :, None, :]
    rotary = tensor[..., :ROT]
    even_part = rotary[..., 0::2]
    odd_part = rotary[..., 1::2]
    rotated = jnp.stack([even_part * cosine - odd_part * sine_part, odd_part * cosine + even_part * sine_part], axis=-1)
    return jnp.concatenate([rotated.reshape(rotary.shape), tensor[..., ROT:]], axis=-1)

def reference(hidden_in, norm_gain, norm_shift, attend_weight, output_weight, up_weight, up_bias, down_weight, down_bias, key_cache, value_cache, cached_len):
    score_scale = HD ** (-0.5)
    normed = layer_norm(hidden_in, norm_gain, norm_shift).astype(jnp.bfloat16)
    projected = jnp.dot(normed, attend_weight.reshape(D, 3 * HEADS * HD), preferred_element_type=jnp.float32)
    projected = projected.reshape(REQS, GROUP, 3, HEADS, HD)
    positions = cached_len[:, None] + jnp.arange(GROUP, dtype=jnp.int32)[None, :]
    queries = rotate_pairs(projected[:, :, 0], positions).astype(jnp.bfloat16)
    keys_new = rotate_pairs(projected[:, :, 1], positions).astype(jnp.bfloat16)
    values_new = projected[:, :, 2].astype(jnp.bfloat16)

    def one_request(packed):
        query_rows, fresh_keys, fresh_values, old_keys, old_values, length = packed
        old_keys = old_keys.reshape(CMAX, HEADS, HD).astype(jnp.float32)
        old_values = old_values.reshape(CMAX, HEADS, HD).astype(jnp.float32)
        query_float = query_rows.astype(jnp.float32)
        cache_scores = jnp.einsum('chd,phd->hcp', query_float, old_keys) * score_scale
        cache_scores = jnp.where(jnp.arange(CMAX, dtype=jnp.int32)[None, None, :] < length, cache_scores, -jnp.inf)
        group_scores = jnp.einsum('chd,khd->hck', query_float, fresh_keys.astype(jnp.float32)) * score_scale
        causal = jnp.arange(GROUP)[:, None] >= jnp.arange(GROUP)[None, :]
        group_scores = jnp.where(causal[None], group_scores, -jnp.inf)
        scores = jnp.concatenate([cache_scores, group_scores], axis=-1)
        top_score = lax.optimization_barrier(jnp.max(scores, axis=-1, keepdims=True))
        expo = jnp.exp(scores - top_score)
        weight_sum = lax.optimization_barrier(jnp.sum(expo, axis=-1))
        rounded = lax.optimization_barrier(expo.astype(jnp.bfloat16))
        weights = rounded.astype(jnp.float32)
        every_value = jnp.concatenate([old_values, fresh_values.astype(jnp.float32)], axis=0)
        context = jnp.einsum('hck,khd->chd', weights, every_value) / jnp.transpose(weight_sum)[:, :, None]
        return context.astype(jnp.bfloat16).reshape(GROUP, HEADS * HD)
    context = lax.map(one_request, (queries, keys_new, values_new, key_cache, value_cache, cached_len))
    context = context.reshape(TOKENS, HEADS * HD)
    attended = jnp.dot(context, output_weight, preferred_element_type=jnp.float32)
    upward = jnp.dot(normed, up_weight, preferred_element_type=jnp.float32) + up_bias
    active = jax.nn.gelu(upward, approximate=True).astype(jnp.bfloat16)
    downward = jnp.dot(active, down_weight, preferred_element_type=jnp.float32)
    hidden_out = (hidden_in.astype(jnp.float32) + (attended + downward) + down_bias).astype(jnp.bfloat16)
    return (hidden_out, keys_new.reshape(REQS, GROUP, HEADS * HD), values_new.reshape(REQS, GROUP, HEADS * HD))
```

```python
import functools

import jax
import jax.numpy as jnp
from jax import lax
from jax.experimental import pallas as pl
from jax.experimental.pallas import tpu as pltpu
from jax.sharding import PartitionSpec as P

HD = 256
ROT = 64
GROUP = 128
BLOCK = 128
LANES = 128


epsilon = 1e-05
very_low = -1e30
f32 = jnp.float32
bf16 = jnp.bfloat16


def params(mib):
    return pltpu.CompilerParams(vmem_limit_bytes=mib * 1024 * 1024)


def cost():
    return pl.CostEstimate(flops=1024, bytes_accessed=1024, transcendentals=0)


def norm_kernel(count, split, order_ref, *refs):
    *pieces, affine_ref, out_ref = refs[: len(refs) - split]
    sent = refs[len(refs) - split :]
    total = out_ref.shape[1]
    width = total // count
    floats = [
        piece[:, start : start + width].astype(f32)
        for piece in pieces
        for start in range(0, piece.shape[1], width)
    ]
    mean = sum(jnp.sum(part, axis=-1, keepdims=True) for part in floats) / total
    floats = [part - mean for part in floats]
    spread = sum(jnp.sum(part * part, axis=-1, keepdims=True) for part in floats) / total
    inverse = lax.rsqrt(spread + epsilon)
    for k, part in enumerate(floats):
        columns = pl.ds(pl.multiple_of(order_ref[k] * width, width), width)
        out_ref[:, columns] = (
            part * inverse * affine_ref[:1, columns] + affine_ref[1:, columns]
        ).astype(bf16)
    if split:
        half = total // 2
        sent[0][...] = out_ref[:, pl.ds(pl.multiple_of(order_ref[count] * half, half), half)]


def norm_call(order, count, pieces, affine, split=False):
    rows = pieces[0].shape[0]
    total = affine.shape[1]
    block = 64
    widths = [total] + [total // 2] * split
    return pl.pallas_call(
        functools.partial(norm_kernel, count, split),
        grid_spec=pltpu.PrefetchScalarGridSpec(
            num_scalar_prefetch=1,
            grid=(rows // block,),
            in_specs=[pl.BlockSpec((block, p.shape[1]), lambda i, order: (i, 0)) for p in pieces]
            + [pl.BlockSpec((2, total), lambda i, order: (0, 0))],
            out_specs=[pl.BlockSpec((block, each), lambda i, order: (i, 0)) for each in widths],
        ),
        out_shape=[jax.ShapeDtypeStruct((rows, each), bf16) for each in widths],
        compiler_params=params(24),
        cost_estimate=cost(),
        name="layer_norm",
    )(order, *pieces, affine)


def project_kernel(heads, x_ref, w_ref, a_ref, b_ref, c_ref, q_ref, k_ref, v_ref):
    step = pl.program_id(0)
    found = jnp.dot(x_ref[...], w_ref[0], preferred_element_type=f32)

    def rotate(out_ref):
        first = found[:, :LANES]
        after = pltpu.roll(first, LANES - 1, 1)
        before = pltpu.roll(first, 1, 1)
        turned = first * a_ref[...] + after * b_ref[...] + before * c_ref[...]
        out_ref[:, :LANES] = turned.astype(bf16)
        out_ref[:, LANES:] = found[:, LANES:].astype(bf16)

    @pl.when(step < heads)
    def _():
        rotate(q_ref)

    @pl.when((step >= heads) & (step < 2 * heads))
    def _():
        rotate(k_ref)

    @pl.when(step >= 2 * heads)
    def _():
        v_ref[...] = found.astype(bf16)


def project_call(normed, weight, positions):
    rows, depth = normed.shape
    local = weight.shape[2]
    heads = local // HD
    lane = jnp.arange(LANES)
    rate = 10000.0 ** (-((lane // 2).astype(f32) * 2.0) / ROT)
    angles = positions.astype(f32)[:, None] * rate
    turns = lane < ROT
    cosine = jnp.where(turns, jnp.cos(angles), 1.0)
    sine = jnp.where(turns, jnp.sin(angles), 0.0)
    even = lane % 2 == 0
    table = pl.BlockSpec((rows, LANES), lambda j: (0, 0))
    out = jax.ShapeDtypeStruct((rows, local), bf16)
    return pl.pallas_call(
        functools.partial(project_kernel, heads),
        grid=(3 * heads,),
        in_specs=[
            pl.BlockSpec((rows, depth), lambda j: (0, 0)),
            pl.BlockSpec((1, depth, HD), lambda j: (j // heads, 0, j % heads)),
            table,
            table,
            table,
        ],
        out_specs=[
            pl.BlockSpec((rows, HD), lambda j: (0, jnp.clip(j, 0, heads - 1))),
            pl.BlockSpec((rows, HD), lambda j: (0, jnp.clip(j - heads, 0, heads - 1))),
            pl.BlockSpec((rows, HD), lambda j: (0, jnp.clip(j - 2 * heads, 0, heads - 1))),
        ],
        out_shape=[out, out, out],
        compiler_params=params(45),
        cost_estimate=cost(),
        name="projections",
    )(normed, weight, cosine, jnp.where(even, -sine, 0.0), jnp.where(even, 0.0, sine))


def attend_kernel(heads, len_ref, q_ref, kn_ref, vn_ref, kc_ref, vc_ref, out_ref):
    length = len_ref[pl.program_id(0)]
    slots = kc_ref.shape[1]
    contract = (((1,), (1,)), ((), ()))
    scale = HD ** (-0.5)
    filled = lax.broadcasted_iota(jnp.int32, (GROUP, slots), 1) < length
    causal = lax.broadcasted_iota(jnp.int32, (GROUP, GROUP), 0) >= lax.broadcasted_iota(
        jnp.int32, (GROUP, GROUP), 1
    )
    for head in range(heads):
        columns = slice(head * HD, (head + 1) * HD)
        query = q_ref[:, columns]
        old = lax.dot_general(query, kc_ref[0, :, columns], contract, preferred_element_type=f32)
        new = lax.dot_general(query, kn_ref[:, columns], contract, preferred_element_type=f32)
        old = jnp.where(filled, old * scale, very_low)
        new = jnp.where(causal, new * scale, very_low)
        top = jnp.maximum(
            jnp.max(old, axis=-1, keepdims=True), jnp.max(new, axis=-1, keepdims=True)
        )
        old = jnp.exp(old - top)
        new = jnp.exp(new - top)
        total = jnp.sum(old, axis=-1, keepdims=True) + jnp.sum(new, axis=-1, keepdims=True)
        weighted = jnp.dot(
            old.astype(bf16), vc_ref[0, :, columns], preferred_element_type=f32
        ) + jnp.dot(new.astype(bf16), vn_ref[:, columns], preferred_element_type=f32)
        out_ref[:, columns] = (weighted / total).astype(bf16)


def attend_call(lengths, query, new_key, new_value, key_cache, value_cache):
    requests, slots, local = key_cache.shape
    fresh = pl.BlockSpec((GROUP, local), lambda r, lengths: (r, 0))
    cached = pl.BlockSpec((1, slots, local), lambda r, lengths: (r, 0, 0))
    return pl.pallas_call(
        functools.partial(attend_kernel, local // HD),
        grid_spec=pltpu.PrefetchScalarGridSpec(
            num_scalar_prefetch=1,
            grid=(requests,),
            in_specs=[fresh, fresh, fresh, cached, cached],
            out_specs=fresh,
        ),
        out_shape=jax.ShapeDtypeStruct((requests * GROUP, local), bf16),
        compiler_params=params(28),
        cost_estimate=cost(),
        name="attention",
    )(lengths, query, new_key, new_value, key_cache, value_cache)


def up_kernel(depths, spots_ref, x_ref, *refs):
    weights, (bias_ref, out_ref) = refs[: len(depths)], refs[len(depths) :]
    total = bias_ref[...] + jnp.zeros(out_ref.shape, f32)
    for k, depth in enumerate(depths):
        columns = pl.ds(pl.multiple_of(spots_ref[k] * LANES, LANES), depth)
        total += jnp.dot(x_ref[:, columns], weights[k][...], preferred_element_type=f32)
    out_ref[...] = jax.nn.gelu(total, approximate=True).astype(bf16)


def up_call(spots, normed, weights, bias):
    rows, depth = normed.shape
    width = weights[0].shape[1]
    depths = [weight.shape[0] for weight in weights]
    block = 256
    return pl.pallas_call(
        functools.partial(up_kernel, depths),
        grid_spec=pltpu.PrefetchScalarGridSpec(
            num_scalar_prefetch=1,
            grid=(width // block,),
            in_specs=[pl.BlockSpec((rows, depth), lambda n, spots: (0, 0))]
            + [pl.BlockSpec((part, block), lambda n, spots: (0, n)) for part in depths]
            + [pl.BlockSpec((1, block), lambda n, spots: (0, n))],
            out_specs=pl.BlockSpec((rows, block), lambda n, spots: (0, n)),
        ),
        out_shape=jax.ShapeDtypeStruct((rows, width), bf16),
        compiler_params=params(40),
        cost_estimate=cost(),
        name="up_and_gelu",
    )(spots, normed, *weights, bias[None])


def up_half_kernel(spots_ref, rows_ref, w0, w1, w2, w3, out_ref, x_ref):
    depth = w0.shape[0]

    @pl.when(pl.program_id(0) == 0)
    def _():
        for k in range(4):
            columns = pl.ds(pl.multiple_of(spots_ref[k] * depth, depth), depth)
            x_ref[:, k * depth : (k + 1) * depth] = rows_ref[:, columns]

    weight = jnp.concatenate([w0[...], w1[...], w2[...], w3[...]], axis=0)
    out_ref[...] = jnp.dot(x_ref[...], weight, preferred_element_type=f32).astype(out_ref.dtype)


def up_half_call(spots, x, weights, start, stop, dtype):
    rows = x.shape[0]
    width = stop - start
    depth = 4 * weights[0].shape[0]
    block = 256
    steps = width // block
    first = start // block
    in_specs = [pl.BlockSpec(x.shape, lambda n, spots: (0, 0))] + [
        pl.BlockSpec((w.shape[0], block), lambda n, spots: (0, first + n)) for w in weights
    ]
    return pl.pallas_call(
        up_half_kernel,
        grid_spec=pltpu.PrefetchScalarGridSpec(
            num_scalar_prefetch=1,
            grid=(steps,),
            in_specs=in_specs,
            out_specs=pl.BlockSpec((rows, block), lambda n, spots: (0, n)),
            scratch_shapes=[pltpu.VMEM((rows, depth), bf16)],
        ),
        out_shape=jax.ShapeDtypeStruct((rows, width), dtype),
        compiler_params=params(28),
        cost_estimate=cost(),
        name="up_half",
    )(spots, x, *weights)


def gelu_kernel(keep_ref, bias_ref, *refs):
    came, out_ref = refs[:-1], refs[-1]
    start = 0
    for ref in came:
        columns = slice(start, start + ref.shape[1])
        start += ref.shape[1]
        upward = keep_ref[:, columns] + ref[...].astype(f32) + bias_ref[:, columns]
        out_ref[:, columns] = jax.nn.gelu(upward, approximate=True).astype(bf16)


def gelu_call(keep, came, bias):
    rows, width = keep.shape
    block = 64
    whole = pl.BlockSpec((block, width), lambda i: (i, 0))
    return pl.pallas_call(
        gelu_kernel,
        grid=(rows // block,),
        in_specs=[whole, pl.BlockSpec((1, width), lambda i: (0, 0))]
        + [pl.BlockSpec((block, part.shape[1]), lambda i: (i, 0)) for part in came],
        out_specs=whole,
        out_shape=jax.ShapeDtypeStruct((rows, width), bf16),
        compiler_params=params(12),
        cost_estimate=cost(),
        name="gelu",
    )(keep, bias[None], *came)


def down_kernel(place_ref, a0, a1, c0, c1, v0, v1, v2, v3, o0, o1, o2, o3, own_ref, hold_ref, send_ref, total):
    step = pl.program_id(0)
    steps = pl.num_programs(0)
    rows, width = a0.shape[0], v0.shape[1]

    @pl.when(step == 0)
    def _():
        weight = jnp.concatenate([o0[...], o1[...], o2[...], o3[...]], axis=1)
        total[:rows] = jnp.dot(c0[...], weight, preferred_element_type=f32)
        total[rows:] = jnp.dot(c1[...], weight, preferred_element_type=f32)

    weight = jnp.concatenate([v0[...], v1[...], v2[...], v3[...]], axis=1)
    total[:rows] += jnp.dot(a0[...], weight, preferred_element_type=f32)
    total[rows:] += jnp.dot(a1[...], weight, preferred_element_type=f32)

    @pl.when(step == steps - 1)
    def _():
        for k in range(4):
            columns = slice(k * width, (k + 1) * width)

            @pl.when(place_ref[4 + k] == 0)
            def _():
                own_ref[...] = total[:, columns]

            @pl.when(place_ref[4 + k] == 1)
            def _():
                send_ref[: 2 * rows] = total[:, columns].astype(bf16)

            @pl.when(place_ref[4 + k] == 2)
            def _():
                hold_ref[...] = total[:, columns]

            @pl.when(place_ref[4 + k] == 3)
            def _():
                send_ref[2 * rows :] = total[:, columns].astype(bf16)


def down_call(place, active, context, weights, out_weight, start, width):
    rows, depth = active[0].shape
    local = context[0].shape[1]
    steps = 4
    part = depth // steps
    per = out_weight.shape[1] // 8 // width
    in_specs = [pl.BlockSpec((rows, part), lambda s, place: (0, s))] * 2
    in_specs += [pl.BlockSpec((rows, local), lambda s, place: (0, 0))] * 2
    for _, column in weights:
        in_specs.append(pl.BlockSpec((part, width), lambda s, place, column=column: (s, column)))
    for k in range(4):
        in_specs.append(
            pl.BlockSpec(
                (local, width), lambda s, place, k=k: (0, place[k] * per + start // width)
            )
        )
    result = pl.BlockSpec((2 * rows, width), lambda s, place: (0, 0))
    double = pl.BlockSpec((4 * rows, width), lambda s, place: (0, 0))
    return pl.pallas_call(
        down_kernel,
        grid_spec=pltpu.PrefetchScalarGridSpec(
            num_scalar_prefetch=1,
            grid=(steps,),
            in_specs=in_specs,
            out_specs=[result, result, double],
            scratch_shapes=[pltpu.VMEM((2 * rows, 4 * width), f32)],
        ),
        out_shape=[jax.ShapeDtypeStruct((2 * rows, width), f32)] * 2
        + [jax.ShapeDtypeStruct((4 * rows, width), bf16)],
        compiler_params=params(24),
        cost_estimate=cost(),
        name="down_and_output",
    )(place, *active, *context, *[w for w, _ in weights], *[out_weight] * 4)


def sum_kernel(own_ref, hold_ref, came_ref, kept_ref, send_ref):
    rows = own_ref.shape[0]
    kept_ref[...] = own_ref[...] + came_ref[:rows].astype(f32)
    send_ref[...] = (hold_ref[...] + came_ref[rows:].astype(f32)).astype(bf16)


def sum_call(own, hold, came):
    return pl.pallas_call(
        sum_kernel,
        out_shape=[
            jax.ShapeDtypeStruct(own.shape, f32),
            jax.ShapeDtypeStruct(own.shape, bf16),
        ],
        compiler_params=params(12),
        cost_estimate=cost(),
        name="sum_near",
    )(own, hold, came)


def join_kernel(widths, *refs):
    keep_ref, send_ref = refs[-2:]
    rows = keep_ref.shape[0]
    start = 0
    for piece, width in enumerate(widths):
        summed = refs[2 * piece][...] + refs[2 * piece + 1][...].astype(f32)
        keep_ref[:, start : start + width] = summed[:rows]
        send_ref[:, start : start + width] = summed[rows:]
        start += width


def join_call(pieces):
    widths = [piece[0].shape[1] for piece in pieces]
    rows = pieces[0][0].shape[0] // 2
    out = jax.ShapeDtypeStruct((rows, sum(widths)), f32)
    return pl.pallas_call(
        functools.partial(join_kernel, widths),
        out_shape=[out, out],
        compiler_params=params(12),
        cost_estimate=cost(),
        name="sum_far",
    )(*[array for piece in pieces for array in piece])


def close_kernel(side_ref, hidden_ref, bias_ref, own_ref, other_ref, out_ref):
    width = own_ref.shape[1]
    for source, side in ((own_ref, side_ref[0]), (other_ref, 1 - side_ref[0])):
        columns = pl.ds(pl.multiple_of(side * width, width), width)
        out_ref[:, columns] = (
            hidden_ref[:, columns].astype(f32) + source[...] + bias_ref[:, columns]
        ).astype(bf16)


def close_call(side, hidden, bias, own, other):
    return pl.pallas_call(
        close_kernel,
        in_specs=[pl.BlockSpec(memory_space=pltpu.SMEM)]
        + [pl.BlockSpec(memory_space=pltpu.VMEM)] * 4,
        out_shape=jax.ShapeDtypeStruct(hidden.shape, bf16),
        compiler_params=params(12),
        cost_estimate=cost(),
        name="final_sum",
    )(side, hidden, bias[None], own, other)


CORE, X, Y = 1, 2, 4


def swap(value, axis, size, mask):
    return lax.ppermute(value, axis, [(i, i ^ mask) for i in range(size)])


def after(value, earlier):
    return lax.optimization_barrier((value, earlier))[0]


def body_small(
    hidden_in,
    norm_gain,
    norm_shift,
    attend_weight,
    output_weight,
    up_weight,
    up_bias,
    down_weight,
    down_bias,
    key_cache,
    value_cache,
    cached_len,
):
    over_req = functools.partial(swap, axis="req", size=8)
    over_head = functools.partial(swap, axis="head", size=4)
    me = lax.axis_index("req").astype(jnp.int32)
    line = lax.axis_index("head").astype(jnp.int32)
    side = me & 1
    chips = jnp.arange(4, dtype=jnp.int32)
    batch_size = key_cache.shape[0]
    local_width = output_weight.shape[0]

    far = over_head(hidden_in, mask=2)
    near = over_head(hidden_in, mask=1)
    up_x = over_req(up_weight, mask=X)
    down_y = over_req(down_weight, mask=Y)
    up_core = over_req(up_weight, mask=CORE)
    last = over_head(far, mask=1)
    pair = jnp.concatenate([hidden_in, near], axis=1)
    affine = jnp.stack([norm_gain, norm_shift])
    last, pair, affine = lax.optimization_barrier((last, pair, affine))

    order = jnp.concatenate([line ^ chips, (1 - (me >> 2))[None]])
    normed, for_other = norm_call(order, 4, [pair, far, last], affine, split=True)
    normed_other = over_req(for_other, mask=Y)
    up_x, up_core, down_y, normed_next = lax.optimization_barrier((up_x, up_core, down_y, normed))
    up_x_core = over_req(up_x, mask=CORE)
    down_x = over_req(after(down_weight, up_x), mask=X)

    half = down_weight.shape[1] // 2
    quarter = half // 2
    forward_y = [down_y[:, k * quarter : (k + 1) * quarter] for k in range(2)]
    diagonal = [over_req(forward_y[0], mask=X)]
    normed_next, forward_y = lax.optimization_barrier((normed_next, forward_y))

    positions = (cached_len[:, None] + jnp.arange(GROUP, dtype=jnp.int32)[None, :]).reshape(-1)
    query, new_key, new_value = project_call(
        normed_next, attend_weight.transpose(1, 0, 2), positions
    )

    blocks = me ^ jnp.array([0, X, CORE, X | CORE], jnp.int32)
    weights = [up_weight, up_x, up_core, up_x_core]
    units = up_weight.shape[1]
    keep = up_half_call(blocks, after(normed, query), weights, 0, units, f32)
    other = after(normed_other, keep)
    came = []
    cut = units * 5 // 8
    for start, stop in ((0, cut), (cut, units)):
        send = up_half_call(blocks & 3, other, weights, start, stop, bf16)
        came.append(over_req(send, mask=Y))
        other = after(other, send)

    query = after(query, other)
    context = attend_call(cached_len, query, new_key, new_value, key_cache, value_cache)
    context_other = over_req(context, mask=CORE)

    came, context_other, diagonal[0] = lax.optimization_barrier((came, context_other, diagonal[0]))
    diagonal.append(over_req(after(forward_y[1], diagonal[0]), mask=X))
    forward_x = [down_x[:, half + k * quarter : half + (k + 1) * quarter] for k in range(2)]
    forward_x = after(forward_x, came)
    diagonal += [over_req(part, mask=Y) for part in forward_x]

    active = gelu_call(keep, came, up_bias)
    active_other = over_req(active, mask=CORE)

    blocks = me ^ (2 * chips)
    place = jnp.concatenate([blocks, line ^ (blocks >> 1)])
    results, behind = {}, []
    previous = None
    rows = active, active_other
    for k in (0, 2, 1, 3):
        if len(behind) == 2:
            rows = after(rows, behind.pop(0))
        own, hold, send = down_call(
            place,
            rows,
            (context, context_other),
            [(down_weight, k), (down_x, k), (down_y, k), (diagonal[k], 0)],
            output_weight,
            k * quarter,
            quarter,
        )
        came = over_head(send, mask=1)
        if previous is not None:
            came = after(came, previous)
        own, second = sum_call(own, hold, came)
        behind.append(second)
        previous = over_head(second, mask=2)
        results[k] = own, previous
    results = [results[k] for k in range(4)]
    own, send = join_call(results)
    other = over_req(send, mask=CORE)
    hidden_out = close_call(side[None], hidden_in, down_bias, own, other)
    shape = (batch_size, GROUP, local_width)
    return hidden_out, new_key.reshape(shape), new_value.reshape(shape)


def body_any(
    hidden_in,
    norm_gain,
    norm_shift,
    attend_weight,
    output_weight,
    up_weight,
    up_bias,
    down_weight,
    down_bias,
    key_cache,
    value_cache,
    cached_len,
):
    batch_size = key_cache.shape[0]
    local_width = output_weight.shape[0]
    gathered = lax.all_gather(hidden_in, "head", axis=1, tiled=True)
    affine = jnp.stack([norm_gain, norm_shift])
    (normed,) = norm_call(jnp.zeros((1,), jnp.int32), 1, [gathered], affine)
    positions = (cached_len[:, None] + jnp.arange(GROUP, dtype=jnp.int32)[None, :]).reshape(-1)
    query, new_key, new_value = project_call(
        normed, attend_weight.transpose(1, 0, 2), positions
    )
    context = attend_call(cached_len, query, new_key, new_value, key_cache, value_cache)
    attended = jnp.dot(context, output_weight, preferred_element_type=f32)
    up_whole = lax.all_gather(up_weight, "req", axis=0, tiled=True)
    active = up_call(jnp.zeros((1,), jnp.int32), normed, [up_whole], up_bias)
    downward = jnp.dot(
        active,
        lax.all_gather(down_weight, "req", axis=1, tiled=True),
        preferred_element_type=f32,
    )
    summed = lax.psum_scatter(
        (attended + downward).astype(bf16), "head", scatter_dimension=1, tiled=True
    ).astype(f32)
    hidden_out = (hidden_in.astype(f32) + summed + down_bias).astype(bf16)
    shape = (batch_size, GROUP, local_width)
    return hidden_out, new_key.reshape(shape), new_value.reshape(shape)


def solution(mesh):
    small = mesh.shape["req"] == 8 and mesh.shape["head"] == 4
    placed = (
        P("req", "head"),
        P(),
        P(),
        P(None, None, "head"),
        P("head", None),
        P("req", "head"),
        P("head"),
        P("head", "req"),
        P("head"),
        P("req", None, "head"),
        P("req", None, "head"),
        P("req"),
    )
    return jax.shard_map(
        body_small if small else body_any,
        mesh=mesh,
        in_specs=placed,
        out_specs=(P("req", "head"), P("req", None, "head"), P("req", None, "head")),
        check_vma=False,
    )
```

```python
import functools

import jax
import jax.numpy as jnp
from jax import lax
from jax.experimental import pallas as pl
from jax.experimental.pallas import tpu as pltpu
from jax.sharding import PartitionSpec as P

HD = 256
ROT = 64
GROUP = 128
BLOCK = 128
LANES = 128


epsilon = 1e-05
very_low = -1e30
f32 = jnp.float32
bf16 = jnp.bfloat16


def params(mib):
    return pltpu.CompilerParams(vmem_limit_bytes=mib * 1024 * 1024)


def cost():
    return pl.CostEstimate(flops=1024, bytes_accessed=1024, transcendentals=0)


def norm_kernel(count, split, order_ref, *refs):
    *pieces, affine_ref, out_ref = refs[: len(refs) - split]
    sent = refs[len(refs) - split :]
    total = out_ref.shape[1]
    width = total // count
    floats = [
        piece[:, start : start + width].astype(f32)
        for piece in pieces
        for start in range(0, piece.shape[1], width)
    ]
    mean = sum(jnp.sum(part, axis=-1, keepdims=True) for part in floats) / total
    floats = [part - mean for part in floats]
    spread = sum(jnp.sum(part * part, axis=-1, keepdims=True) for part in floats) / total
    inverse = lax.rsqrt(spread + epsilon)
    for k, part in enumerate(floats):
        columns = pl.ds(pl.multiple_of(order_ref[k] * width, width), width)
        out_ref[:, columns] = (
            part * inverse * affine_ref[:1, columns] + affine_ref[1:, columns]
        ).astype(bf16)
    if split:
        half = total // 2
        sent[0][...] = out_ref[:, pl.ds(pl.multiple_of(order_ref[count] * half, half), half)]


def norm_call(order, count, pieces, affine, split=False):
    rows = pieces[0].shape[0]
    total = affine.shape[1]
    block = 64
    widths = [total] + [total // 2] * split
    return pl.pallas_call(
        functools.partial(norm_kernel, count, split),
        grid_spec=pltpu.PrefetchScalarGridSpec(
            num_scalar_prefetch=1,
            grid=(rows // block,),
            in_specs=[pl.BlockSpec((block, p.shape[1]), lambda i, order: (i, 0)) for p in pieces]
            + [pl.BlockSpec((2, total), lambda i, order: (0, 0))],
            out_specs=[pl.BlockSpec((block, each), lambda i, order: (i, 0)) for each in widths],
        ),
        out_shape=[jax.ShapeDtypeStruct((rows, each), bf16) for each in widths],
        compiler_params=params(24),
        cost_estimate=cost(),
        name="layer_norm",
    )(order, *pieces, affine)


def project_kernel(heads, x_ref, w_ref, a_ref, b_ref, c_ref, q_ref, k_ref, v_ref):
    step = pl.program_id(0)
    found = jnp.dot(x_ref[...], w_ref[0], preferred_element_type=f32)

    def rotate(out_ref):
        first = found[:, :LANES]
        after = pltpu.roll(first, LANES - 1, 1)
        before = pltpu.roll(first, 1, 1)
        turned = first * a_ref[...] + after * b_ref[...] + before * c_ref[...]
        out_ref[:, :LANES] = turned.astype(bf16)
        out_ref[:, LANES:] = found[:, LANES:].astype(bf16)

    @pl.when(step < heads)
    def _():
        rotate(q_ref)

    @pl.when((step >= heads) & (step < 2 * heads))
    def _():
        rotate(k_ref)

    @pl.when(step >= 2 * heads)
    def _():
        v_ref[...] = found.astype(bf16)


def project_call(normed, weight, positions):
    rows, depth = normed.shape
    local = weight.shape[2]
    heads = local // HD
    lane = jnp.arange(LANES)
    rate = 10000.0 ** (-((lane // 2).astype(f32) * 2.0) / ROT)
    angles = positions.astype(f32)[:, None] * rate
    turns = lane < ROT
    cosine = jnp.where(turns, jnp.cos(angles), 1.0)
    sine = jnp.where(turns, jnp.sin(angles), 0.0)
    even = lane % 2 == 0
    table = pl.BlockSpec((rows, LANES), lambda j: (0, 0))
    out = jax.ShapeDtypeStruct((rows, local), bf16)
    return pl.pallas_call(
        functools.partial(project_kernel, heads),
        grid=(3 * heads,),
        in_specs=[
            pl.BlockSpec((rows, depth), lambda j: (0, 0)),
            pl.BlockSpec((1, depth, HD), lambda j: (j // heads, 0, j % heads)),
            table,
            table,
            table,
        ],
        out_specs=[
            pl.BlockSpec((rows, HD), lambda j: (0, jnp.clip(j, 0, heads - 1))),
            pl.BlockSpec((rows, HD), lambda j: (0, jnp.clip(j - heads, 0, heads - 1))),
            pl.BlockSpec((rows, HD), lambda j: (0, jnp.clip(j - 2 * heads, 0, heads - 1))),
        ],
        out_shape=[out, out, out],
        compiler_params=params(45),
        cost_estimate=cost(),
        name="projections",
    )(normed, weight, cosine, jnp.where(even, -sine, 0.0), jnp.where(even, 0.0, sine))


def attend_kernel(heads, len_ref, q_ref, kn_ref, vn_ref, kc_ref, vc_ref, out_ref):
    length = len_ref[pl.program_id(0)]
    slots = kc_ref.shape[1]
    contract = (((1,), (1,)), ((), ()))
    scale = HD ** (-0.5)
    filled = lax.broadcasted_iota(jnp.int32, (GROUP, slots), 1) < length
    causal = lax.broadcasted_iota(jnp.int32, (GROUP, GROUP), 0) >= lax.broadcasted_iota(
        jnp.int32, (GROUP, GROUP), 1
    )
    for head in range(heads):
        columns = slice(head * HD, (head + 1) * HD)
        query = q_ref[:, columns]
        old = lax.dot_general(query, kc_ref[0, :, columns], contract, preferred_element_type=f32)
        new = lax.dot_general(query, kn_ref[:, columns], contract, preferred_element_type=f32)
        old = jnp.where(filled, old * scale, very_low)
        new = jnp.where(causal, new * scale, very_low)
        top = jnp.maximum(
            jnp.max(old, axis=-1, keepdims=True), jnp.max(new, axis=-1, keepdims=True)
        )
        old = jnp.exp(old - top)
        new = jnp.exp(new - top)
        total = jnp.sum(old, axis=-1, keepdims=True) + jnp.sum(new, axis=-1, keepdims=True)
        weighted = jnp.dot(
            old.astype(bf16), vc_ref[0, :, columns], preferred_element_type=f32
        ) + jnp.dot(new.astype(bf16), vn_ref[:, columns], preferred_element_type=f32)
        out_ref[:, columns] = (weighted / total).astype(bf16)


def attend_call(lengths, query, new_key, new_value, key_cache, value_cache):
    requests, slots, local = key_cache.shape
    fresh = pl.BlockSpec((GROUP, local), lambda r, lengths: (r, 0))
    cached = pl.BlockSpec((1, slots, local), lambda r, lengths: (r, 0, 0))
    return pl.pallas_call(
        functools.partial(attend_kernel, local // HD),
        grid_spec=pltpu.PrefetchScalarGridSpec(
            num_scalar_prefetch=1,
            grid=(requests,),
            in_specs=[fresh, fresh, fresh, cached, cached],
            out_specs=fresh,
        ),
        out_shape=jax.ShapeDtypeStruct((requests * GROUP, local), bf16),
        compiler_params=params(28),
        cost_estimate=cost(),
        name="attention",
    )(lengths, query, new_key, new_value, key_cache, value_cache)


def up_kernel(depths, spots_ref, x_ref, *refs):
    weights, (bias_ref, out_ref) = refs[: len(depths)], refs[len(depths) :]
    total = bias_ref[...] + jnp.zeros(out_ref.shape, f32)
    for k, depth in enumerate(depths):
        columns = pl.ds(pl.multiple_of(spots_ref[k] * LANES, LANES), depth)
        total += jnp.dot(x_ref[:, columns], weights[k][...], preferred_element_type=f32)
    out_ref[...] = jax.nn.gelu(total, approximate=True).astype(bf16)


def up_call(spots, normed, weights, bias):
    rows, depth = normed.shape
    width = weights[0].shape[1]
    depths = [weight.shape[0] for weight in weights]
    block = 256
    return pl.pallas_call(
        functools.partial(up_kernel, depths),
        grid_spec=pltpu.PrefetchScalarGridSpec(
            num_scalar_prefetch=1,
            grid=(width // block,),
            in_specs=[pl.BlockSpec((rows, depth), lambda n, spots: (0, 0))]
            + [pl.BlockSpec((part, block), lambda n, spots: (0, n)) for part in depths]
            + [pl.BlockSpec((1, block), lambda n, spots: (0, n))],
            out_specs=pl.BlockSpec((rows, block), lambda n, spots: (0, n)),
        ),
        out_shape=jax.ShapeDtypeStruct((rows, width), bf16),
        compiler_params=params(40),
        cost_estimate=cost(),
        name="up_and_gelu",
    )(spots, normed, *weights, bias[None])


def up_half_kernel(spots_ref, rows_ref, w0, w1, w2, w3, out_ref, x_ref):
    depth = w0.shape[0]

    @pl.when(pl.program_id(0) == 0)
    def _():
        for k in range(4):
            columns = pl.ds(pl.multiple_of(spots_ref[k] * depth, depth), depth)
            x_ref[:, k * depth : (k + 1) * depth] = rows_ref[:, columns]

    weight = jnp.concatenate([w0[...], w1[...], w2[...], w3[...]], axis=0)
    out_ref[...] = jnp.dot(x_ref[...], weight, preferred_element_type=f32).astype(out_ref.dtype)


def up_half_call(spots, x, weights, start, stop, dtype):
    rows = x.shape[0]
    width = stop - start
    depth = 4 * weights[0].shape[0]
    block = 256
    steps = width // block
    first = start // block
    in_specs = [pl.BlockSpec(x.shape, lambda n, spots: (0, 0))] + [
        pl.BlockSpec((w.shape[0], block), lambda n, spots: (0, first + n)) for w in weights
    ]
    return pl.pallas_call(
        up_half_kernel,
        grid_spec=pltpu.PrefetchScalarGridSpec(
            num_scalar_prefetch=1,
            grid=(steps,),
            in_specs=in_specs,
            out_specs=pl.BlockSpec((rows, block), lambda n, spots: (0, n)),
            scratch_shapes=[pltpu.VMEM((rows, depth), bf16)],
        ),
        out_shape=jax.ShapeDtypeStruct((rows, width), dtype),
        compiler_params=params(28),
        cost_estimate=cost(),
        name="up_half",
    )(spots, x, *weights)


def gelu_kernel(keep_ref, bias_ref, *refs):
    came, out_ref = refs[:-1], refs[-1]
    start = 0
    for ref in came:
        columns = slice(start, start + ref.shape[1])
        start += ref.shape[1]
        upward = keep_ref[:, columns] + ref[...].astype(f32) + bias_ref[:, columns]
        out_ref[:, columns] = jax.nn.gelu(upward, approximate=True).astype(bf16)


def gelu_call(keep, came, bias):
    rows, width = keep.shape
    block = 64
    whole = pl.BlockSpec((block, width), lambda i: (i, 0))
    return pl.pallas_call(
        gelu_kernel,
        grid=(rows // block,),
        in_specs=[whole, pl.BlockSpec((1, width), lambda i: (0, 0))]
        + [pl.BlockSpec((block, part.shape[1]), lambda i: (i, 0)) for part in came],
        out_specs=whole,
        out_shape=jax.ShapeDtypeStruct((rows, width), bf16),
        compiler_params=params(12),
        cost_estimate=cost(),
        name="gelu",
    )(keep, bias[None], *came)


def down_kernel(place_ref, a0, a1, c0, c1, v0, v1, v2, v3, o0, o1, o2, o3, own_ref, hold_ref, send_ref, total):
    step = pl.program_id(0)
    steps = pl.num_programs(0)
    rows, width = a0.shape[0], v0.shape[1]

    @pl.when(step == 0)
    def _():
        weight = jnp.concatenate([o0[...], o1[...], o2[...], o3[...]], axis=1)
        context = jnp.concatenate([c0[...], c1[...]], axis=0)
        total[...] = jnp.dot(context, weight, preferred_element_type=f32)

    weight = jnp.concatenate([v0[...], v1[...], v2[...], v3[...]], axis=1)
    active = jnp.concatenate([a0[...], a1[...]], axis=0)
    total[...] += jnp.dot(active, weight, preferred_element_type=f32)

    @pl.when(step == steps - 1)
    def _():
        for k in range(4):
            columns = slice(k * width, (k + 1) * width)

            @pl.when(place_ref[4 + k] == 0)
            def _():
                own_ref[...] = total[:, columns]

            @pl.when(place_ref[4 + k] == 1)
            def _():
                send_ref[: 2 * rows] = total[:, columns].astype(bf16)

            @pl.when(place_ref[4 + k] == 2)
            def _():
                hold_ref[...] = total[:, columns]

            @pl.when(place_ref[4 + k] == 3)
            def _():
                send_ref[2 * rows :] = total[:, columns].astype(bf16)


def down_call(place, active, context, weights, out_weight, start, width):
    rows, depth = active[0].shape
    local = context[0].shape[1]
    steps = 4
    part = depth // steps
    per = out_weight.shape[1] // 8 // width
    in_specs = [pl.BlockSpec((rows, part), lambda s, place: (0, s))] * 2
    in_specs += [pl.BlockSpec((rows, local), lambda s, place: (0, 0))] * 2
    for _, column in weights:
        in_specs.append(pl.BlockSpec((part, width), lambda s, place, column=column: (s, column)))
    for k in range(4):
        in_specs.append(
            pl.BlockSpec(
                (local, width), lambda s, place, k=k: (0, place[k] * per + start // width)
            )
        )
    result = pl.BlockSpec((2 * rows, width), lambda s, place: (0, 0))
    double = pl.BlockSpec((4 * rows, width), lambda s, place: (0, 0))
    return pl.pallas_call(
        down_kernel,
        grid_spec=pltpu.PrefetchScalarGridSpec(
            num_scalar_prefetch=1,
            grid=(steps,),
            in_specs=in_specs,
            out_specs=[result, result, double],
            scratch_shapes=[pltpu.VMEM((2 * rows, 4 * width), f32)],
        ),
        out_shape=[jax.ShapeDtypeStruct((2 * rows, width), f32)] * 2
        + [jax.ShapeDtypeStruct((4 * rows, width), bf16)],
        compiler_params=params(24),
        cost_estimate=cost(),
        name="down_and_output",
    )(place, *active, *context, *[w for w, _ in weights], *[out_weight] * 4)


def sum_kernel(own_ref, hold_ref, came_ref, kept_ref, send_ref):
    rows = own_ref.shape[0]
    kept_ref[...] = own_ref[...] + came_ref[:rows].astype(f32)
    send_ref[...] = (hold_ref[...] + came_ref[rows:].astype(f32)).astype(bf16)


def sum_call(own, hold, came):
    return pl.pallas_call(
        sum_kernel,
        out_shape=[
            jax.ShapeDtypeStruct(own.shape, f32),
            jax.ShapeDtypeStruct(own.shape, bf16),
        ],
        compiler_params=params(12),
        cost_estimate=cost(),
        name="sum_near",
    )(own, hold, came)


def join_kernel(widths, *refs):
    keep_ref, send_ref = refs[-2:]
    rows = keep_ref.shape[0]
    start = 0
    for piece, width in enumerate(widths):
        summed = refs[2 * piece][...] + refs[2 * piece + 1][...].astype(f32)
        keep_ref[:, start : start + width] = summed[:rows]
        send_ref[:, start : start + width] = summed[rows:]
        start += width


def join_call(pieces):
    widths = [piece[0].shape[1] for piece in pieces]
    rows = pieces[0][0].shape[0] // 2
    out = jax.ShapeDtypeStruct((rows, sum(widths)), f32)
    return pl.pallas_call(
        functools.partial(join_kernel, widths),
        out_shape=[out, out],
        compiler_params=params(12),
        cost_estimate=cost(),
        name="sum_far",
    )(*[array for piece in pieces for array in piece])


def close_kernel(side_ref, hidden_ref, bias_ref, own_ref, other_ref, out_ref):
    width = own_ref.shape[1]
    for source, side in ((own_ref, side_ref[0]), (other_ref, 1 - side_ref[0])):
        columns = pl.ds(pl.multiple_of(side * width, width), width)
        out_ref[:, columns] = (
            hidden_ref[:, columns].astype(f32) + source[...] + bias_ref[:, columns]
        ).astype(bf16)


def close_call(side, hidden, bias, own, other):
    return pl.pallas_call(
        close_kernel,
        in_specs=[pl.BlockSpec(memory_space=pltpu.SMEM)]
        + [pl.BlockSpec(memory_space=pltpu.VMEM)] * 4,
        out_shape=jax.ShapeDtypeStruct(hidden.shape, bf16),
        compiler_params=params(12),
        cost_estimate=cost(),
        name="final_sum",
    )(side, hidden, bias[None], own, other)


CORE, X, Y = 1, 2, 4


def swap(value, axis, size, mask):
    return lax.ppermute(value, axis, [(i, i ^ mask) for i in range(size)])


def after(value, earlier):
    return lax.optimization_barrier((value, earlier))[0]


def body_small(
    hidden_in,
    norm_gain,
    norm_shift,
    attend_weight,
    output_weight,
    up_weight,
    up_bias,
    down_weight,
    down_bias,
    key_cache,
    value_cache,
    cached_len,
):
    over_req = functools.partial(swap, axis="req", size=8)
    over_head = functools.partial(swap, axis="head", size=4)
    me = lax.axis_index("req").astype(jnp.int32)
    line = lax.axis_index("head").astype(jnp.int32)
    side = me & 1
    chips = jnp.arange(4, dtype=jnp.int32)
    batch_size = key_cache.shape[0]
    local_width = output_weight.shape[0]

    far = over_head(hidden_in, mask=2)
    near = over_head(hidden_in, mask=1)
    up_x = over_req(up_weight, mask=X)
    down_y = over_req(down_weight, mask=Y)
    up_core = over_req(up_weight, mask=CORE)
    last = over_head(far, mask=1)
    pair = jnp.concatenate([hidden_in, near], axis=1)
    affine = jnp.stack([norm_gain, norm_shift])
    last, pair, affine = lax.optimization_barrier((last, pair, affine))

    order = jnp.concatenate([line ^ chips, (1 - (me >> 2))[None]])
    normed, for_other = norm_call(order, 4, [pair, far, last], affine, split=True)
    normed_other = over_req(for_other, mask=Y)
    up_x, up_core, down_y, normed_next = lax.optimization_barrier((up_x, up_core, down_y, normed))
    up_x_core = over_req(up_x, mask=CORE)
    down_x = over_req(after(down_weight, up_x), mask=X)

    half = down_weight.shape[1] // 2
    quarter = half // 2
    forward_y = [down_y[:, k * quarter : (k + 1) * quarter] for k in range(2)]
    diagonal = [over_req(forward_y[0], mask=X)]
    normed_next, forward_y = lax.optimization_barrier((normed_next, forward_y))

    positions = (cached_len[:, None] + jnp.arange(GROUP, dtype=jnp.int32)[None, :]).reshape(-1)
    query, new_key, new_value = project_call(
        normed_next, attend_weight.transpose(1, 0, 2), positions
    )

    blocks = me ^ jnp.array([0, X, CORE, X | CORE], jnp.int32)
    weights = [up_weight, up_x, up_core, up_x_core]
    units = up_weight.shape[1]
    keep = up_half_call(blocks, after(normed, query), weights, 0, units, f32)
    other = after(normed_other, keep)
    came = []
    cut = units * 5 // 8
    for start, stop in ((0, cut), (cut, units)):
        send = up_half_call(blocks & 3, other, weights, start, stop, bf16)
        came.append(over_req(send, mask=Y))
        other = after(other, send)

    query = after(query, other)
    context = attend_call(cached_len, query, new_key, new_value, key_cache, value_cache)
    context_other = over_req(context, mask=CORE)

    came, context_other, diagonal[0] = lax.optimization_barrier((came, context_other, diagonal[0]))
    diagonal.append(over_req(after(forward_y[1], diagonal[0]), mask=X))
    forward_x = [down_x[:, half + k * quarter : half + (k + 1) * quarter] for k in range(2)]
    forward_x = after(forward_x, came)
    diagonal += [over_req(part, mask=Y) for part in forward_x]

    active = gelu_call(keep, came, up_bias)
    active_other = over_req(active, mask=CORE)

    blocks = me ^ (2 * chips)
    place = jnp.concatenate([blocks, line ^ (blocks >> 1)])
    results, far_sums = {}, []
    rows = active, active_other
    for place_in_order, k in enumerate((0, 1, 2, 3)):
        own, hold, send = down_call(
            place,
            rows,
            (context, context_other),
            [(down_weight, k), (down_x, k), (down_y, k), (diagonal[k], 0)],
            output_weight,
            k * quarter,
            quarter,
        )
        came = over_head(send, mask=1)
        if place_in_order:
            came = after(came, far_sums[max(0, place_in_order - 2)])
        own, second = sum_call(own, hold, came)
        if place_in_order == 0:
            rows = after(rows, second)
        far_sums.append(over_head(second, mask=2))
        if place_in_order == 1:
            rows = after(rows, far_sums[0])
        results[k] = own, far_sums[-1]
    results = [results[k] for k in range(4)]
    own, send = join_call(results)
    other = over_req(send, mask=CORE)
    hidden_out = close_call(side[None], hidden_in, down_bias, own, other)
    shape = (batch_size, GROUP, local_width)
    return hidden_out, new_key.reshape(shape), new_value.reshape(shape)


def body_any(
    hidden_in,
    norm_gain,
    norm_shift,
    attend_weight,
    output_weight,
    up_weight,
    up_bias,
    down_weight,
    down_bias,
    key_cache,
    value_cache,
    cached_len,
):
    batch_size = key_cache.shape[0]
    local_width = output_weight.shape[0]
    gathered = lax.all_gather(hidden_in, "head", axis=1, tiled=True)
    affine = jnp.stack([norm_gain, norm_shift])
    (normed,) = norm_call(jnp.zeros((1,), jnp.int32), 1, [gathered], affine)
    positions = (cached_len[:, None] + jnp.arange(GROUP, dtype=jnp.int32)[None, :]).reshape(-1)
    query, new_key, new_value = project_call(
        normed, attend_weight.transpose(1, 0, 2), positions
    )
    context = attend_call(cached_len, query, new_key, new_value, key_cache, value_cache)
    attended = jnp.dot(context, output_weight, preferred_element_type=f32)
    up_whole = lax.all_gather(up_weight, "req", axis=0, tiled=True)
    active = up_call(jnp.zeros((1,), jnp.int32), normed, [up_whole], up_bias)
    downward = jnp.dot(
        active,
        lax.all_gather(down_weight, "req", axis=1, tiled=True),
        preferred_element_type=f32,
    )
    summed = lax.psum_scatter(
        (attended + downward).astype(bf16), "head", scatter_dimension=1, tiled=True
    ).astype(f32)
    hidden_out = (hidden_in.astype(f32) + summed + down_bias).astype(bf16)
    shape = (batch_size, GROUP, local_width)
    return hidden_out, new_key.reshape(shape), new_value.reshape(shape)


def solution(mesh):
    small = mesh.shape["req"] == 8 and mesh.shape["head"] == 4
    placed = (
        P("req", "head"),
        P(),
        P(),
        P(None, None, "head"),
        P("head", None),
        P("req", "head"),
        P("head"),
        P("head", "req"),
        P("head"),
        P("req", None, "head"),
        P("req", None, "head"),
        P("req"),
    )
    return jax.shard_map(
        body_small if small else body_any,
        mesh=mesh,
        in_specs=placed,
        out_specs=(P("req", "head"), P("req", None, "head"), P("req", None, "head")),
        check_vma=False,
    )
```

```python
import functools

import jax
import jax.numpy as jnp
from jax import lax
from jax.experimental import pallas as pl
from jax.experimental.pallas import tpu as pltpu
from jax.sharding import PartitionSpec as P

HD = 256
ROT = 64
GROUP = 128
BLOCK = 128
LANES = 128


epsilon = 1e-05
very_low = -1e30
f32 = jnp.float32
bf16 = jnp.bfloat16


def params(mib):
    return pltpu.CompilerParams(vmem_limit_bytes=mib * 1024 * 1024)


def cost():
    return pl.CostEstimate(flops=1024, bytes_accessed=1024, transcendentals=0)


def norm_kernel(count, split, order_ref, *refs):
    *pieces, affine_ref, out_ref = refs[: len(refs) - split]
    sent = refs[len(refs) - split :]
    total = out_ref.shape[1]
    width = total // count
    floats = [
        piece[:, start : start + width].astype(f32)
        for piece in pieces
        for start in range(0, piece.shape[1], width)
    ]
    mean = sum(jnp.sum(part, axis=-1, keepdims=True) for part in floats) / total
    floats = [part - mean for part in floats]
    spread = sum(jnp.sum(part * part, axis=-1, keepdims=True) for part in floats) / total
    inverse = lax.rsqrt(spread + epsilon)
    for k, part in enumerate(floats):
        columns = pl.ds(pl.multiple_of(order_ref[k] * width, width), width)
        out_ref[:, columns] = (
            part * inverse * affine_ref[:1, columns] + affine_ref[1:, columns]
        ).astype(bf16)
    if split:
        half = total // 2
        sent[0][...] = out_ref[:, pl.ds(pl.multiple_of(order_ref[count] * half, half), half)]


def norm_call(order, count, pieces, affine, split=False):
    rows = pieces[0].shape[0]
    total = affine.shape[1]
    block = 64
    widths = [total] + [total // 2] * split
    return pl.pallas_call(
        functools.partial(norm_kernel, count, split),
        grid_spec=pltpu.PrefetchScalarGridSpec(
            num_scalar_prefetch=1,
            grid=(rows // block,),
            in_specs=[pl.BlockSpec((block, p.shape[1]), lambda i, order: (i, 0)) for p in pieces]
            + [pl.BlockSpec((2, total), lambda i, order: (0, 0))],
            out_specs=[pl.BlockSpec((block, each), lambda i, order: (i, 0)) for each in widths],
        ),
        out_shape=[jax.ShapeDtypeStruct((rows, each), bf16) for each in widths],
        compiler_params=params(24),
        cost_estimate=cost(),
        name="layer_norm",
    )(order, *pieces, affine)


def project_kernel(heads, x_ref, w_ref, a_ref, b_ref, c_ref, q_ref, k_ref, v_ref):
    step = pl.program_id(0)
    found = jnp.dot(x_ref[...], w_ref[0], preferred_element_type=f32)

    def rotate(out_ref):
        first = found[:, :LANES]
        after = pltpu.roll(first, LANES - 1, 1)
        before = pltpu.roll(first, 1, 1)
        turned = first * a_ref[...] + after * b_ref[...] + before * c_ref[...]
        out_ref[:, :LANES] = turned.astype(bf16)
        out_ref[:, LANES:] = found[:, LANES:].astype(bf16)

    @pl.when(step < heads)
    def _():
        rotate(q_ref)

    @pl.when((step >= heads) & (step < 2 * heads))
    def _():
        rotate(k_ref)

    @pl.when(step >= 2 * heads)
    def _():
        v_ref[...] = found.astype(bf16)


def project_call(normed, weight, positions):
    rows, depth = normed.shape
    local = weight.shape[2]
    heads = local // HD
    lane = jnp.arange(LANES)
    rate = 10000.0 ** (-((lane // 2).astype(f32) * 2.0) / ROT)
    angles = positions.astype(f32)[:, None] * rate
    turns = lane < ROT
    cosine = jnp.where(turns, jnp.cos(angles), 1.0)
    sine = jnp.where(turns, jnp.sin(angles), 0.0)
    even = lane % 2 == 0
    table = pl.BlockSpec((rows, LANES), lambda j: (0, 0))
    out = jax.ShapeDtypeStruct((rows, local), bf16)
    return pl.pallas_call(
        functools.partial(project_kernel, heads),
        grid=(3 * heads,),
        in_specs=[
            pl.BlockSpec((rows, depth), lambda j: (0, 0)),
            pl.BlockSpec((1, depth, HD), lambda j: (j // heads, 0, j % heads)),
            table,
            table,
            table,
        ],
        out_specs=[
            pl.BlockSpec((rows, HD), lambda j: (0, jnp.clip(j, 0, heads - 1))),
            pl.BlockSpec((rows, HD), lambda j: (0, jnp.clip(j - heads, 0, heads - 1))),
            pl.BlockSpec((rows, HD), lambda j: (0, jnp.clip(j - 2 * heads, 0, heads - 1))),
        ],
        out_shape=[out, out, out],
        compiler_params=params(45),
        cost_estimate=cost(),
        name="projections",
    )(normed, weight, cosine, jnp.where(even, -sine, 0.0), jnp.where(even, 0.0, sine))


def attend_kernel(heads, len_ref, q_ref, kn_ref, vn_ref, kc_ref, vc_ref, out_ref):
    length = len_ref[pl.program_id(0)]
    slots = kc_ref.shape[1]
    contract = (((1,), (1,)), ((), ()))
    scale = HD ** (-0.5)
    filled = lax.broadcasted_iota(jnp.int32, (GROUP, slots), 1) < length
    causal = lax.broadcasted_iota(jnp.int32, (GROUP, GROUP), 0) >= lax.broadcasted_iota(
        jnp.int32, (GROUP, GROUP), 1
    )
    for head in range(heads):
        columns = slice(head * HD, (head + 1) * HD)
        query = q_ref[:, columns]
        old = lax.dot_general(query, kc_ref[0, :, columns], contract, preferred_element_type=f32)
        new = lax.dot_general(query, kn_ref[:, columns], contract, preferred_element_type=f32)
        old = jnp.where(filled, old * scale, very_low)
        new = jnp.where(causal, new * scale, very_low)
        top = jnp.maximum(
            jnp.max(old, axis=-1, keepdims=True), jnp.max(new, axis=-1, keepdims=True)
        )
        old = jnp.exp(old - top)
        new = jnp.exp(new - top)
        total = jnp.sum(old, axis=-1, keepdims=True) + jnp.sum(new, axis=-1, keepdims=True)
        weighted = jnp.dot(
            old.astype(bf16), vc_ref[0, :, columns], preferred_element_type=f32
        ) + jnp.dot(new.astype(bf16), vn_ref[:, columns], preferred_element_type=f32)
        out_ref[:, columns] = (weighted / total).astype(bf16)


def attend_call(lengths, query, new_key, new_value, key_cache, value_cache):
    requests, slots, local = key_cache.shape
    fresh = pl.BlockSpec((GROUP, local), lambda r, lengths: (r, 0))
    cached = pl.BlockSpec((1, slots, local), lambda r, lengths: (r, 0, 0))
    return pl.pallas_call(
        functools.partial(attend_kernel, local // HD),
        grid_spec=pltpu.PrefetchScalarGridSpec(
            num_scalar_prefetch=1,
            grid=(requests,),
            in_specs=[fresh, fresh, fresh, cached, cached],
            out_specs=fresh,
        ),
        out_shape=jax.ShapeDtypeStruct((requests * GROUP, local), bf16),
        compiler_params=params(28),
        cost_estimate=cost(),
        name="attention",
    )(lengths, query, new_key, new_value, key_cache, value_cache)


def up_kernel(depths, spots_ref, x_ref, *refs):
    weights, (bias_ref, out_ref) = refs[: len(depths)], refs[len(depths) :]
    total = bias_ref[...] + jnp.zeros(out_ref.shape, f32)
    for k, depth in enumerate(depths):
        columns = pl.ds(pl.multiple_of(spots_ref[k] * LANES, LANES), depth)
        total += jnp.dot(x_ref[:, columns], weights[k][...], preferred_element_type=f32)
    out_ref[...] = jax.nn.gelu(total, approximate=True).astype(bf16)


def up_call(spots, normed, weights, bias):
    rows, depth = normed.shape
    width = weights[0].shape[1]
    depths = [weight.shape[0] for weight in weights]
    block = 256
    return pl.pallas_call(
        functools.partial(up_kernel, depths),
        grid_spec=pltpu.PrefetchScalarGridSpec(
            num_scalar_prefetch=1,
            grid=(width // block,),
            in_specs=[pl.BlockSpec((rows, depth), lambda n, spots: (0, 0))]
            + [pl.BlockSpec((part, block), lambda n, spots: (0, n)) for part in depths]
            + [pl.BlockSpec((1, block), lambda n, spots: (0, n))],
            out_specs=pl.BlockSpec((rows, block), lambda n, spots: (0, n)),
        ),
        out_shape=jax.ShapeDtypeStruct((rows, width), bf16),
        compiler_params=params(40),
        cost_estimate=cost(),
        name="up_and_gelu",
    )(spots, normed, *weights, bias[None])


def up_half_kernel(spots_ref, rows_ref, w0, w1, w2, w3, out_ref, x_ref):
    depth = w0.shape[0]

    @pl.when(pl.program_id(0) == 0)
    def _():
        for k in range(4):
            columns = pl.ds(pl.multiple_of(spots_ref[k] * depth, depth), depth)
            x_ref[:, k * depth : (k + 1) * depth] = rows_ref[:, columns]

    weight = jnp.concatenate([w0[...], w1[...], w2[...], w3[...]], axis=0)
    out_ref[...] = jnp.dot(x_ref[...], weight, preferred_element_type=f32).astype(out_ref.dtype)


def up_half_call(spots, x, weights, start, stop, dtype):
    rows = x.shape[0]
    width = stop - start
    depth = 4 * weights[0].shape[0]
    block = 256
    steps = width // block
    first = start // block
    in_specs = [pl.BlockSpec(x.shape, lambda n, spots: (0, 0))] + [
        pl.BlockSpec((w.shape[0], block), lambda n, spots: (0, first + n)) for w in weights
    ]
    return pl.pallas_call(
        up_half_kernel,
        grid_spec=pltpu.PrefetchScalarGridSpec(
            num_scalar_prefetch=1,
            grid=(steps,),
            in_specs=in_specs,
            out_specs=pl.BlockSpec((rows, block), lambda n, spots: (0, n)),
            scratch_shapes=[pltpu.VMEM((rows, depth), bf16)],
        ),
        out_shape=jax.ShapeDtypeStruct((rows, width), dtype),
        compiler_params=params(28),
        cost_estimate=cost(),
        name="up_half",
    )(spots, x, *weights)


def gelu_kernel(keep_ref, bias_ref, *refs):
    came, out_ref = refs[:-1], refs[-1]
    start = 0
    for ref in came:
        columns = slice(start, start + ref.shape[1])
        start += ref.shape[1]
        upward = keep_ref[:, columns] + ref[...].astype(f32) + bias_ref[:, columns]
        out_ref[:, columns] = jax.nn.gelu(upward, approximate=True).astype(bf16)


def gelu_call(keep, came, bias):
    rows, width = keep.shape
    block = 64
    whole = pl.BlockSpec((block, width), lambda i: (i, 0))
    return pl.pallas_call(
        gelu_kernel,
        grid=(rows // block,),
        in_specs=[whole, pl.BlockSpec((1, width), lambda i: (0, 0))]
        + [pl.BlockSpec((block, part.shape[1]), lambda i: (i, 0)) for part in came],
        out_specs=whole,
        out_shape=jax.ShapeDtypeStruct((rows, width), bf16),
        compiler_params=params(12),
        cost_estimate=cost(),
        name="gelu",
    )(keep, bias[None], *came)


def down_kernel(place_ref, a0, a1, c0, c1, v0, v1, v2, v3, o0, o1, o2, o3, own_ref, hold_ref, send_ref, total):
    step = pl.program_id(0)
    steps = pl.num_programs(0)
    rows, width = a0.shape[0], v0.shape[1]

    weight = jnp.concatenate([v0[...], v1[...], v2[...], v3[...]], axis=1)
    active = jnp.concatenate([a0[...], a1[...]], axis=0)
    part = jnp.dot(active, weight, preferred_element_type=f32)

    @pl.when(step == 0)
    def _():
        out_weight = jnp.concatenate([o0[...], o1[...], o2[...], o3[...]], axis=1)
        context = jnp.concatenate([c0[...], c1[...]], axis=0)
        total[...] = part + jnp.dot(context, out_weight, preferred_element_type=f32)

    @pl.when((step > 0) & (step < steps - 1))
    def _():
        total[...] += part

    @pl.when(step == steps - 1)
    def _():
        for k in range(4):
            columns = slice(k * width, (k + 1) * width)
            found = total[:, columns] + part[:, columns]

            @pl.when(place_ref[4 + k] == 0)
            def _():
                own_ref[...] = found

            @pl.when(place_ref[4 + k] == 1)
            def _():
                send_ref[: 2 * rows] = found.astype(bf16)

            @pl.when(place_ref[4 + k] == 2)
            def _():
                hold_ref[...] = found

            @pl.when(place_ref[4 + k] == 3)
            def _():
                send_ref[2 * rows :] = found.astype(bf16)


def down_call(place, active, context, weights, out_weight, start, width):
    rows, depth = active[0].shape
    local = context[0].shape[1]
    steps = 2
    part = depth // steps
    per = out_weight.shape[1] // 8 // width
    in_specs = [pl.BlockSpec((rows, part), lambda s, place: (0, s))] * 2
    in_specs += [pl.BlockSpec((rows, local), lambda s, place: (0, 0))] * 2
    for _, column in weights:
        in_specs.append(pl.BlockSpec((part, width), lambda s, place, column=column: (s, column)))
    for k in range(4):
        in_specs.append(
            pl.BlockSpec(
                (local, width), lambda s, place, k=k: (0, place[k] * per + start // width)
            )
        )
    result = pl.BlockSpec((2 * rows, width), lambda s, place: (0, 0))
    double = pl.BlockSpec((4 * rows, width), lambda s, place: (0, 0))
    return pl.pallas_call(
        down_kernel,
        grid_spec=pltpu.PrefetchScalarGridSpec(
            num_scalar_prefetch=1,
            grid=(steps,),
            in_specs=in_specs,
            out_specs=[result, result, double],
            scratch_shapes=[pltpu.VMEM((2 * rows, 4 * width), f32)],
        ),
        out_shape=[jax.ShapeDtypeStruct((2 * rows, width), f32)] * 2
        + [jax.ShapeDtypeStruct((4 * rows, width), bf16)],
        compiler_params=params(24),
        cost_estimate=cost(),
        name="down_and_output",
    )(place, *active, *context, *[w for w, _ in weights], *[out_weight] * 4)


def sum_kernel(own_ref, hold_ref, came_ref, kept_ref, send_ref):
    rows = own_ref.shape[0]
    kept_ref[...] = own_ref[...] + came_ref[:rows].astype(f32)
    send_ref[...] = (hold_ref[...] + came_ref[rows:].astype(f32)).astype(bf16)


def sum_call(own, hold, came):
    return pl.pallas_call(
        sum_kernel,
        out_shape=[
            jax.ShapeDtypeStruct(own.shape, f32),
            jax.ShapeDtypeStruct(own.shape, bf16),
        ],
        compiler_params=params(12),
        cost_estimate=cost(),
        name="sum_near",
    )(own, hold, came)


def join_kernel(widths, *refs):
    keep_ref, send_ref = refs[-2:]
    rows = keep_ref.shape[0]
    start = 0
    for piece, width in enumerate(widths):
        summed = refs[2 * piece][...] + refs[2 * piece + 1][...].astype(f32)
        keep_ref[:, start : start + width] = summed[:rows]
        send_ref[:, start : start + width] = summed[rows:]
        start += width


def join_call(pieces):
    widths = [piece[0].shape[1] for piece in pieces]
    rows = pieces[0][0].shape[0] // 2
    out = jax.ShapeDtypeStruct((rows, sum(widths)), f32)
    return pl.pallas_call(
        functools.partial(join_kernel, widths),
        out_shape=[out, out],
        compiler_params=params(12),
        cost_estimate=cost(),
        name="sum_far",
    )(*[array for piece in pieces for array in piece])


def close_kernel(side_ref, hidden_ref, bias_ref, own_ref, other_ref, out_ref):
    width = own_ref.shape[1]
    for source, side in ((own_ref, side_ref[0]), (other_ref, 1 - side_ref[0])):
        columns = pl.ds(pl.multiple_of(side * width, width), width)
        out_ref[:, columns] = (
            hidden_ref[:, columns].astype(f32) + source[...] + bias_ref[:, columns]
        ).astype(bf16)


def close_call(side, hidden, bias, own, other):
    return pl.pallas_call(
        close_kernel,
        in_specs=[pl.BlockSpec(memory_space=pltpu.SMEM)]
        + [pl.BlockSpec(memory_space=pltpu.VMEM)] * 4,
        out_shape=jax.ShapeDtypeStruct(hidden.shape, bf16),
        compiler_params=params(12),
        cost_estimate=cost(),
        name="final_sum",
    )(side, hidden, bias[None], own, other)


CORE, X, Y = 1, 2, 4


def swap(value, axis, size, mask):
    return lax.ppermute(value, axis, [(i, i ^ mask) for i in range(size)])


def after(value, earlier):
    return lax.optimization_barrier((value, earlier))[0]


def body_small(
    hidden_in,
    norm_gain,
    norm_shift,
    attend_weight,
    output_weight,
    up_weight,
    up_bias,
    down_weight,
    down_bias,
    key_cache,
    value_cache,
    cached_len,
):
    over_req = functools.partial(swap, axis="req", size=8)
    over_head = functools.partial(swap, axis="head", size=4)
    me = lax.axis_index("req").astype(jnp.int32)
    line = lax.axis_index("head").astype(jnp.int32)
    side = me & 1
    chips = jnp.arange(4, dtype=jnp.int32)
    batch_size = key_cache.shape[0]
    local_width = output_weight.shape[0]

    far = over_head(hidden_in, mask=2)
    near = over_head(hidden_in, mask=1)
    up_x = over_req(up_weight, mask=X)
    down_y = over_req(down_weight, mask=Y)
    up_core = over_req(up_weight, mask=CORE)
    last = over_head(far, mask=1)
    pair = jnp.concatenate([hidden_in, near], axis=1)
    affine = jnp.stack([norm_gain, norm_shift])
    last, pair, affine = lax.optimization_barrier((last, pair, affine))

    order = jnp.concatenate([line ^ chips, (1 - (me >> 2))[None]])
    normed, for_other = norm_call(order, 4, [pair, far, last], affine, split=True)
    normed_other = over_req(for_other, mask=Y)
    up_x, up_core, normed_next = lax.optimization_barrier((up_x, up_core, normed))
    up_x_core = over_req(up_x, mask=CORE)
    down_x = over_req(after(down_weight, up_x), mask=X)
    down_y, normed_next = lax.optimization_barrier((down_y, normed_next))

    half = down_weight.shape[1] // 2
    quarter = half // 2
    forward_y = [down_y[:, k * quarter : (k + 1) * quarter] for k in range(2)]
    diagonal = [over_req(forward_y[0], mask=X)]
    normed_next, forward_y = lax.optimization_barrier((normed_next, forward_y))

    positions = (cached_len[:, None] + jnp.arange(GROUP, dtype=jnp.int32)[None, :]).reshape(-1)
    query, new_key, new_value = project_call(
        normed_next, attend_weight.transpose(1, 0, 2), positions
    )

    blocks = me ^ jnp.array([0, X, CORE, X | CORE], jnp.int32)
    weights = [up_weight, up_x, up_core, up_x_core]
    units = up_weight.shape[1]
    keep = up_half_call(blocks, after(normed, query), weights, 0, units, f32)
    other = after(normed_other, keep)
    came = []
    cuts = [0, units * 5 // 8, units]
    for start, stop in zip(cuts, cuts[1:]):
        send = up_half_call(blocks & 3, other, weights, start, stop, bf16)
        came.append(over_req(send, mask=Y))
        other = after(other, send)

    query = after(query, send)
    context = attend_call(cached_len, query, new_key, new_value, key_cache, value_cache)
    context_other = over_req(context, mask=CORE)

    came, context_other = lax.optimization_barrier((came, context_other))
    diagonal.append(over_req(after(forward_y[1], diagonal[0]), mask=X))
    forward_x = [down_x[:, half + k * quarter : half + (k + 1) * quarter] for k in range(2)]
    forward_x = after(forward_x, came)
    diagonal += [over_req(part, mask=Y) for part in forward_x]

    active = gelu_call(keep, came, up_bias)
    active_other = over_req(after(active, diagonal[0]), mask=CORE)

    blocks = me ^ (2 * chips)
    place = jnp.concatenate([blocks, line ^ (blocks >> 1)])
    results, far_sums = {}, []
    rows = active, active_other
    for place_in_order, k in enumerate((0, 1, 2, 3)):
        own, hold, send = down_call(
            place,
            rows,
            (context, context_other),
            [(down_weight, k), (down_x, k), (down_y, k), (diagonal[k], 0)],
            output_weight,
            k * quarter,
            quarter,
        )
        came = over_head(send, mask=1)
        if place_in_order:
            came = after(came, far_sums[max(0, place_in_order - 2)])
        own, second = sum_call(own, hold, came)
        if place_in_order == 0:
            rows = after(rows, second)
        far_sums.append(over_head(second, mask=2))
        if place_in_order == 1:
            rows = after(rows, far_sums[0])
        results[k] = own, far_sums[-1]
    results = [results[k] for k in range(4)]
    own, send = join_call(results)
    other = over_req(send, mask=CORE)
    hidden_out = close_call(side[None], hidden_in, down_bias, own, other)
    shape = (batch_size, GROUP, local_width)
    return hidden_out, new_key.reshape(shape), new_value.reshape(shape)


def body_any(
    hidden_in,
    norm_gain,
    norm_shift,
    attend_weight,
    output_weight,
    up_weight,
    up_bias,
    down_weight,
    down_bias,
    key_cache,
    value_cache,
    cached_len,
):
    batch_size = key_cache.shape[0]
    local_width = output_weight.shape[0]
    gathered = lax.all_gather(hidden_in, "head", axis=1, tiled=True)
    affine = jnp.stack([norm_gain, norm_shift])
    (normed,) = norm_call(jnp.zeros((1,), jnp.int32), 1, [gathered], affine)
    positions = (cached_len[:, None] + jnp.arange(GROUP, dtype=jnp.int32)[None, :]).reshape(-1)
    query, new_key, new_value = project_call(
        normed, attend_weight.transpose(1, 0, 2), positions
    )
    context = attend_call(cached_len, query, new_key, new_value, key_cache, value_cache)
    attended = jnp.dot(context, output_weight, preferred_element_type=f32)
    up_whole = lax.all_gather(up_weight, "req", axis=0, tiled=True)
    active = up_call(jnp.zeros((1,), jnp.int32), normed, [up_whole], up_bias)
    downward = jnp.dot(
        active,
        lax.all_gather(down_weight, "req", axis=1, tiled=True),
        preferred_element_type=f32,
    )
    summed = lax.psum_scatter(
        (attended + downward).astype(bf16), "head", scatter_dimension=1, tiled=True
    ).astype(f32)
    hidden_out = (hidden_in.astype(f32) + summed + down_bias).astype(bf16)
    shape = (batch_size, GROUP, local_width)
    return hidden_out, new_key.reshape(shape), new_value.reshape(shape)


def solution(mesh):
    small = mesh.shape["req"] == 8 and mesh.shape["head"] == 4
    placed = (
        P("req", "head"),
        P(),
        P(),
        P(None, None, "head"),
        P("head", None),
        P("req", "head"),
        P("head"),
        P("head", "req"),
        P("head"),
        P("req", None, "head"),
        P("req", None, "head"),
        P("req"),
    )
    return jax.shard_map(
        body_small if small else body_any,
        mesh=mesh,
        in_specs=placed,
        out_specs=(P("req", "head"), P("req", None, "head"), P("req", None, "head")),
        check_vma=False,
    )
```

```python
import functools

import jax
import jax.numpy as jnp
from jax import lax
from jax.experimental import pallas as pl
from jax.experimental.pallas import tpu as pltpu
from jax.sharding import PartitionSpec as P

HD = 256
ROT = 64
GROUP = 128
BLOCK = 128
LANES = 128


epsilon = 1e-05
very_low = -1e30
f32 = jnp.float32
bf16 = jnp.bfloat16


def params(mib):
    return pltpu.CompilerParams(vmem_limit_bytes=mib * 1024 * 1024)


def cost():
    return pl.CostEstimate(flops=1024, bytes_accessed=1024, transcendentals=0)


def norm_kernel(count, split, order_ref, *refs):
    *pieces, affine_ref, out_ref = refs[: len(refs) - split]
    sent = refs[len(refs) - split :]
    total = out_ref.shape[1]
    width = total // count
    floats = [
        piece[:, start : start + width].astype(f32)
        for piece in pieces
        for start in range(0, piece.shape[1], width)
    ]
    mean = sum(jnp.sum(part, axis=-1, keepdims=True) for part in floats) / total
    floats = [part - mean for part in floats]
    spread = sum(jnp.sum(part * part, axis=-1, keepdims=True) for part in floats) / total
    inverse = lax.rsqrt(spread + epsilon)
    for k, part in enumerate(floats):
        columns = pl.ds(pl.multiple_of(order_ref[k] * width, width), width)
        out_ref[:, columns] = (
            part * inverse * affine_ref[:1, columns] + affine_ref[1:, columns]
        ).astype(bf16)
    if split:
        half = total // 2
        sent[0][...] = out_ref[:, pl.ds(pl.multiple_of(order_ref[count] * half, half), half)]


def norm_call(order, count, pieces, affine, split=False):
    rows = pieces[0].shape[0]
    total = affine.shape[1]
    block = 64
    widths = [total] + [total // 2] * split
    return pl.pallas_call(
        functools.partial(norm_kernel, count, split),
        grid_spec=pltpu.PrefetchScalarGridSpec(
            num_scalar_prefetch=1,
            grid=(rows // block,),
            in_specs=[pl.BlockSpec((block, p.shape[1]), lambda i, order: (i, 0)) for p in pieces]
            + [pl.BlockSpec((2, total), lambda i, order: (0, 0))],
            out_specs=[pl.BlockSpec((block, each), lambda i, order: (i, 0)) for each in widths],
        ),
        out_shape=[jax.ShapeDtypeStruct((rows, each), bf16) for each in widths],
        compiler_params=params(24),
        cost_estimate=cost(),
        name="layer_norm",
    )(order, *pieces, affine)


def project_kernel(heads, x_ref, w_ref, a_ref, b_ref, c_ref, q_ref, k_ref, v_ref):
    step = pl.program_id(0)
    found = jnp.dot(x_ref[...], w_ref[0], preferred_element_type=f32)

    def rotate(out_ref):
        first = found[:, :LANES]
        after = pltpu.roll(first, LANES - 1, 1)
        before = pltpu.roll(first, 1, 1)
        turned = first * a_ref[...] + after * b_ref[...] + before * c_ref[...]
        out_ref[:, :LANES] = turned.astype(bf16)
        out_ref[:, LANES:] = found[:, LANES:].astype(bf16)

    @pl.when(step < heads)
    def _():
        rotate(q_ref)

    @pl.when((step >= heads) & (step < 2 * heads))
    def _():
        rotate(k_ref)

    @pl.when(step >= 2 * heads)
    def _():
        v_ref[...] = found.astype(bf16)


def project_call(normed, weight, positions):
    rows, depth = normed.shape
    local = weight.shape[2]
    heads = local // HD
    lane = jnp.arange(LANES)
    rate = 10000.0 ** (-((lane // 2).astype(f32) * 2.0) / ROT)
    angles = positions.astype(f32)[:, None] * rate
    turns = lane < ROT
    cosine = jnp.where(turns, jnp.cos(angles), 1.0)
    sine = jnp.where(turns, jnp.sin(angles), 0.0)
    even = lane % 2 == 0
    table = pl.BlockSpec((rows, LANES), lambda j: (0, 0))
    out = jax.ShapeDtypeStruct((rows, local), bf16)
    return pl.pallas_call(
        functools.partial(project_kernel, heads),
        grid=(3 * heads,),
        in_specs=[
            pl.BlockSpec((rows, depth), lambda j: (0, 0)),
            pl.BlockSpec((1, depth, HD), lambda j: (j // heads, 0, j % heads)),
            table,
            table,
            table,
        ],
        out_specs=[
            pl.BlockSpec((rows, HD), lambda j: (0, jnp.clip(j, 0, heads - 1))),
            pl.BlockSpec((rows, HD), lambda j: (0, jnp.clip(j - heads, 0, heads - 1))),
            pl.BlockSpec((rows, HD), lambda j: (0, jnp.clip(j - 2 * heads, 0, heads - 1))),
        ],
        out_shape=[out, out, out],
        compiler_params=params(45),
        cost_estimate=cost(),
        name="projections",
    )(normed, weight, cosine, jnp.where(even, -sine, 0.0), jnp.where(even, 0.0, sine))


def attend_kernel(heads, len_ref, q_ref, kn_ref, vn_ref, kc_ref, vc_ref, out_ref):
    length = len_ref[pl.program_id(0)]
    slots = kc_ref.shape[1]
    contract = (((1,), (1,)), ((), ()))
    scale = HD ** (-0.5)
    filled = lax.broadcasted_iota(jnp.int32, (GROUP, slots), 1) < length
    causal = lax.broadcasted_iota(jnp.int32, (GROUP, GROUP), 0) >= lax.broadcasted_iota(
        jnp.int32, (GROUP, GROUP), 1
    )
    for head in range(heads):
        columns = slice(head * HD, (head + 1) * HD)
        query = q_ref[:, columns]
        old = lax.dot_general(query, kc_ref[0, :, columns], contract, preferred_element_type=f32)
        new = lax.dot_general(query, kn_ref[:, columns], contract, preferred_element_type=f32)
        old = jnp.where(filled, old * scale, very_low)
        new = jnp.where(causal, new * scale, very_low)
        top = jnp.maximum(
            jnp.max(old, axis=-1, keepdims=True), jnp.max(new, axis=-1, keepdims=True)
        )
        old = jnp.exp(old - top)
        new = jnp.exp(new - top)
        total = jnp.sum(old, axis=-1, keepdims=True) + jnp.sum(new, axis=-1, keepdims=True)
        weighted = jnp.dot(
            old.astype(bf16), vc_ref[0, :, columns], preferred_element_type=f32
        ) + jnp.dot(new.astype(bf16), vn_ref[:, columns], preferred_element_type=f32)
        out_ref[:, columns] = (weighted / total).astype(bf16)


def attend_call(lengths, query, new_key, new_value, key_cache, value_cache):
    requests, slots, local = key_cache.shape
    fresh = pl.BlockSpec((GROUP, local), lambda r, lengths: (r, 0))
    cached = pl.BlockSpec((1, slots, local), lambda r, lengths: (r, 0, 0))
    return pl.pallas_call(
        functools.partial(attend_kernel, local // HD),
        grid_spec=pltpu.PrefetchScalarGridSpec(
            num_scalar_prefetch=1,
            grid=(requests,),
            in_specs=[fresh, fresh, fresh, cached, cached],
            out_specs=fresh,
        ),
        out_shape=jax.ShapeDtypeStruct((requests * GROUP, local), bf16),
        compiler_params=params(28),
        cost_estimate=cost(),
        name="attention",
    )(lengths, query, new_key, new_value, key_cache, value_cache)


def up_kernel(depths, spots_ref, x_ref, *refs):
    weights, (bias_ref, out_ref) = refs[: len(depths)], refs[len(depths) :]
    total = bias_ref[...] + jnp.zeros(out_ref.shape, f32)
    for k, depth in enumerate(depths):
        columns = pl.ds(pl.multiple_of(spots_ref[k] * LANES, LANES), depth)
        total += jnp.dot(x_ref[:, columns], weights[k][...], preferred_element_type=f32)
    out_ref[...] = jax.nn.gelu(total, approximate=True).astype(bf16)


def up_call(spots, normed, weights, bias):
    rows, depth = normed.shape
    width = weights[0].shape[1]
    depths = [weight.shape[0] for weight in weights]
    block = 256
    return pl.pallas_call(
        functools.partial(up_kernel, depths),
        grid_spec=pltpu.PrefetchScalarGridSpec(
            num_scalar_prefetch=1,
            grid=(width // block,),
            in_specs=[pl.BlockSpec((rows, depth), lambda n, spots: (0, 0))]
            + [pl.BlockSpec((part, block), lambda n, spots: (0, n)) for part in depths]
            + [pl.BlockSpec((1, block), lambda n, spots: (0, n))],
            out_specs=pl.BlockSpec((rows, block), lambda n, spots: (0, n)),
        ),
        out_shape=jax.ShapeDtypeStruct((rows, width), bf16),
        compiler_params=params(40),
        cost_estimate=cost(),
        name="up_and_gelu",
    )(spots, normed, *weights, bias[None])


def up_half_kernel(spots_ref, rows_ref, w0, w1, w2, w3, out_ref, x_ref):
    depth = w0.shape[0]

    @pl.when(pl.program_id(0) == 0)
    def _():
        for k in range(4):
            columns = pl.ds(pl.multiple_of(spots_ref[k] * depth, depth), depth)
            x_ref[:, k * depth : (k + 1) * depth] = rows_ref[:, columns]

    weight = jnp.concatenate([w0[...], w1[...], w2[...], w3[...]], axis=0)
    out_ref[...] = jnp.dot(x_ref[...], weight, preferred_element_type=f32).astype(out_ref.dtype)


def up_half_call(spots, x, weights, start, stop, dtype):
    rows = x.shape[0]
    width = stop - start
    depth = 4 * weights[0].shape[0]
    block = 256
    steps = width // block
    first = start // block
    in_specs = [pl.BlockSpec(x.shape, lambda n, spots: (0, 0))] + [
        pl.BlockSpec((w.shape[0], block), lambda n, spots: (0, first + n)) for w in weights
    ]
    return pl.pallas_call(
        up_half_kernel,
        grid_spec=pltpu.PrefetchScalarGridSpec(
            num_scalar_prefetch=1,
            grid=(steps,),
            in_specs=in_specs,
            out_specs=pl.BlockSpec((rows, block), lambda n, spots: (0, n)),
            scratch_shapes=[pltpu.VMEM((rows, depth), bf16)],
        ),
        out_shape=jax.ShapeDtypeStruct((rows, width), dtype),
        compiler_params=params(28),
        cost_estimate=cost(),
        name="up_half",
    )(spots, x, *weights)


def gelu_kernel(keep_ref, bias_ref, *refs):
    came, out_ref = refs[:-1], refs[-1]
    start = 0
    for ref in came:
        columns = slice(start, start + ref.shape[1])
        start += ref.shape[1]
        upward = keep_ref[:, columns] + ref[...].astype(f32) + bias_ref[:, columns]
        out_ref[:, columns] = jax.nn.gelu(upward, approximate=True).astype(bf16)


def gelu_call(keep, came, bias):
    rows, width = keep.shape
    block = 64
    whole = pl.BlockSpec((block, width), lambda i: (i, 0))
    return pl.pallas_call(
        gelu_kernel,
        grid=(rows // block,),
        in_specs=[whole, pl.BlockSpec((1, width), lambda i: (0, 0))]
        + [pl.BlockSpec((block, part.shape[1]), lambda i: (i, 0)) for part in came],
        out_specs=whole,
        out_shape=jax.ShapeDtypeStruct((rows, width), bf16),
        compiler_params=params(12),
        cost_estimate=cost(),
        name="gelu",
    )(keep, bias[None], *came)


def down_kernel(place_ref, a0, a1, c0, c1, v0, v1, v2, v3, o0, o1, o2, o3, own_ref, hold_ref, send_ref, total):
    step = pl.program_id(0)
    steps = pl.num_programs(0)
    rows, width = a0.shape[0], v0.shape[1]

    weight = jnp.concatenate([v0[...], v1[...], v2[...], v3[...]], axis=1)
    active = jnp.concatenate([a0[...], a1[...]], axis=0)
    part = jnp.dot(active, weight, preferred_element_type=f32)

    @pl.when(step == 0)
    def _():
        out_weight = jnp.concatenate([o0[...], o1[...], o2[...], o3[...]], axis=1)
        context = jnp.concatenate([c0[...], c1[...]], axis=0)
        total[...] = part + jnp.dot(context, out_weight, preferred_element_type=f32)

    @pl.when((step > 0) & (step < steps - 1))
    def _():
        total[...] += part

    @pl.when(step == steps - 1)
    def _():
        for k in range(4):
            columns = slice(k * width, (k + 1) * width)
            found = total[:, columns] + part[:, columns]

            @pl.when(place_ref[4 + k] == 0)
            def _():
                own_ref[...] = found

            @pl.when(place_ref[4 + k] == 1)
            def _():
                send_ref[: 2 * rows] = found.astype(bf16)

            @pl.when(place_ref[4 + k] == 2)
            def _():
                hold_ref[...] = found

            @pl.when(place_ref[4 + k] == 3)
            def _():
                send_ref[2 * rows :] = found.astype(bf16)


def down_call(place, active, context, weights, out_weight, start, width):
    rows, depth = active[0].shape
    local = context[0].shape[1]
    steps = 2
    part = depth // steps
    per = out_weight.shape[1] // 8 // width
    in_specs = [pl.BlockSpec((rows, part), lambda s, place: (0, s))] * 2
    in_specs += [pl.BlockSpec((rows, local), lambda s, place: (0, 0))] * 2
    for _, column in weights:
        in_specs.append(pl.BlockSpec((part, width), lambda s, place, column=column: (s, column)))
    for k in range(4):
        in_specs.append(
            pl.BlockSpec(
                (local, width), lambda s, place, k=k: (0, place[k] * per + start // width)
            )
        )
    result = pl.BlockSpec((2 * rows, width), lambda s, place: (0, 0))
    double = pl.BlockSpec((4 * rows, width), lambda s, place: (0, 0))
    return pl.pallas_call(
        down_kernel,
        grid_spec=pltpu.PrefetchScalarGridSpec(
            num_scalar_prefetch=1,
            grid=(steps,),
            in_specs=in_specs,
            out_specs=[result, result, double],
            scratch_shapes=[pltpu.VMEM((2 * rows, 4 * width), f32)],
        ),
        out_shape=[jax.ShapeDtypeStruct((2 * rows, width), f32)] * 2
        + [jax.ShapeDtypeStruct((4 * rows, width), bf16)],
        compiler_params=params(24),
        cost_estimate=cost(),
        name="down_and_output",
    )(place, *active, *context, *[w for w, _ in weights], *[out_weight] * 4)


def sum_kernel(own_ref, hold_ref, came_ref, kept_ref, send_ref):
    rows = own_ref.shape[0]
    kept_ref[...] = own_ref[...] + came_ref[:rows].astype(f32)
    send_ref[...] = (hold_ref[...] + came_ref[rows:].astype(f32)).astype(bf16)


def sum_call(own, hold, came):
    return pl.pallas_call(
        sum_kernel,
        out_shape=[
            jax.ShapeDtypeStruct(own.shape, f32),
            jax.ShapeDtypeStruct(own.shape, bf16),
        ],
        compiler_params=params(12),
        cost_estimate=cost(),
        name="sum_near",
    )(own, hold, came)


def join_kernel(widths, *refs):
    keep_ref, send_ref = refs[-2:]
    rows = keep_ref.shape[0]
    start = 0
    for piece, width in enumerate(widths):
        summed = refs[2 * piece][...] + refs[2 * piece + 1][...].astype(f32)
        keep_ref[:, start : start + width] = summed[:rows]
        send_ref[:, start : start + width] = summed[rows:]
        start += width


def join_call(pieces):
    widths = [piece[0].shape[1] for piece in pieces]
    rows = pieces[0][0].shape[0] // 2
    out = jax.ShapeDtypeStruct((rows, sum(widths)), f32)
    return pl.pallas_call(
        functools.partial(join_kernel, widths),
        out_shape=[out, out],
        compiler_params=params(12),
        cost_estimate=cost(),
        name="sum_far",
    )(*[array for piece in pieces for array in piece])


def close_kernel(side_ref, hidden_ref, bias_ref, own_ref, other_ref, out_ref):
    width = own_ref.shape[1]
    for source, side in ((own_ref, side_ref[0]), (other_ref, 1 - side_ref[0])):
        columns = pl.ds(pl.multiple_of(side * width, width), width)
        out_ref[:, columns] = (
            hidden_ref[:, columns].astype(f32) + source[...] + bias_ref[:, columns]
        ).astype(bf16)


def close_call(side, hidden, bias, own, other):
    return pl.pallas_call(
        close_kernel,
        in_specs=[pl.BlockSpec(memory_space=pltpu.SMEM)]
        + [pl.BlockSpec(memory_space=pltpu.VMEM)] * 4,
        out_shape=jax.ShapeDtypeStruct(hidden.shape, bf16),
        compiler_params=params(12),
        cost_estimate=cost(),
        name="final_sum",
    )(side, hidden, bias[None], own, other)


CORE, X, Y = 1, 2, 4


def swap(value, axis, size, mask):
    return lax.ppermute(value, axis, [(i, i ^ mask) for i in range(size)])


def after(value, earlier):
    return lax.optimization_barrier((value, earlier))[0]


def body_small(
    hidden_in,
    norm_gain,
    norm_shift,
    attend_weight,
    output_weight,
    up_weight,
    up_bias,
    down_weight,
    down_bias,
    key_cache,
    value_cache,
    cached_len,
):
    over_req = functools.partial(swap, axis="req", size=8)
    over_head = functools.partial(swap, axis="head", size=4)
    me = lax.axis_index("req").astype(jnp.int32)
    line = lax.axis_index("head").astype(jnp.int32)
    side = me & 1
    chips = jnp.arange(4, dtype=jnp.int32)
    batch_size = key_cache.shape[0]
    local_width = output_weight.shape[0]

    far = over_head(hidden_in, mask=2)
    near = over_head(hidden_in, mask=1)
    up_x = over_req(up_weight, mask=X)
    down_y = over_req(down_weight, mask=Y)
    up_core = over_req(up_weight, mask=CORE)
    last = over_head(far, mask=1)
    pair = jnp.concatenate([hidden_in, near], axis=1)
    affine = jnp.stack([norm_gain, norm_shift])
    last, pair, affine = lax.optimization_barrier((last, pair, affine))

    order = jnp.concatenate([line ^ chips, (1 - (me >> 2))[None]])
    normed, for_other = norm_call(order, 4, [pair, far, last], affine, split=True)
    normed_other = over_req(for_other, mask=Y)
    up_x, up_core, normed_next = lax.optimization_barrier((up_x, up_core, normed))
    up_x_core = over_req(up_x, mask=CORE)
    down_x = over_req(after(down_weight, up_x), mask=X)
    down_y, normed_next = lax.optimization_barrier((down_y, normed_next))

    half = down_weight.shape[1] // 2
    quarter = half // 2
    forward_y = [down_y[:, k * quarter : (k + 1) * quarter] for k in range(2)]
    diagonal = [over_req(forward_y[0], mask=X)]
    normed_next, forward_y = lax.optimization_barrier((normed_next, forward_y))

    positions = (cached_len[:, None] + jnp.arange(GROUP, dtype=jnp.int32)[None, :]).reshape(-1)
    query, new_key, new_value = project_call(
        normed_next, attend_weight.transpose(1, 0, 2), positions
    )

    blocks = me ^ jnp.array([0, X, CORE, X | CORE], jnp.int32)
    weights = [up_weight, up_x, up_core, up_x_core]
    units = up_weight.shape[1]
    keep = up_half_call(blocks, after(normed, query), weights, 0, units, f32)
    other = after(normed_other, keep)
    came = []
    cuts = [0, units * 5 // 8, units]
    for start, stop in zip(cuts, cuts[1:]):
        send = up_half_call(blocks & 3, other, weights, start, stop, bf16)
        came.append(over_req(send, mask=Y))
        other = after(other, send)

    query = after(query, send)
    context = attend_call(cached_len, query, new_key, new_value, key_cache, value_cache)
    context_other = over_req(context, mask=CORE)

    came, context_other = lax.optimization_barrier((came, context_other))
    diagonal.append(over_req(after(forward_y[1], diagonal[0]), mask=X))
    forward_x = [down_x[:, half + k * quarter : half + (k + 1) * quarter] for k in range(2)]
    forward_x = after(forward_x, came)
    diagonal += [over_req(part, mask=Y) for part in forward_x]

    active = gelu_call(keep, came, up_bias)
    active_other = over_req(after(active, diagonal[0]), mask=CORE)

    blocks = me ^ (2 * chips)
    place = jnp.concatenate([blocks, line ^ (blocks >> 1)])
    results, near_sums, far_sums = [], [], []
    rows = active, active_other
    for k in range(4):
        if k >= 2:
            rows = after(rows, near_sums[k - 2])
        if k == 3:
            rows = after(rows, far_sums[0])
        own, hold, send = down_call(
            place,
            rows,
            (context, context_other),
            [(down_weight, k), (down_x, k), (down_y, k), (diagonal[k], 0)],
            output_weight,
            k * quarter,
            quarter,
        )
        rows = after(rows, send)
        came = over_head(send, mask=1)
        if k:
            came = after(came, far_sums[-1])
        own, second = sum_call(own, hold, came)
        near_sums.append(second)
        far_sums.append(over_head(second, mask=2))
        results.append((own, far_sums[-1]))
    own, send = join_call(results)
    other = over_req(send, mask=CORE)
    hidden_out = close_call(side[None], hidden_in, down_bias, own, other)
    shape = (batch_size, GROUP, local_width)
    return hidden_out, new_key.reshape(shape), new_value.reshape(shape)


def body_any(
    hidden_in,
    norm_gain,
    norm_shift,
    attend_weight,
    output_weight,
    up_weight,
    up_bias,
    down_weight,
    down_bias,
    key_cache,
    value_cache,
    cached_len,
):
    batch_size = key_cache.shape[0]
    local_width = output_weight.shape[0]
    gathered = lax.all_gather(hidden_in, "head", axis=1, tiled=True)
    affine = jnp.stack([norm_gain, norm_shift])
    (normed,) = norm_call(jnp.zeros((1,), jnp.int32), 1, [gathered], affine)
    positions = (cached_len[:, None] + jnp.arange(GROUP, dtype=jnp.int32)[None, :]).reshape(-1)
    query, new_key, new_value = project_call(
        normed, attend_weight.transpose(1, 0, 2), positions
    )
    context = attend_call(cached_len, query, new_key, new_value, key_cache, value_cache)
    attended = jnp.dot(context, output_weight, preferred_element_type=f32)
    up_whole = lax.all_gather(up_weight, "req", axis=0, tiled=True)
    active = up_call(jnp.zeros((1,), jnp.int32), normed, [up_whole], up_bias)
    downward = jnp.dot(
        active,
        lax.all_gather(down_weight, "req", axis=1, tiled=True),
        preferred_element_type=f32,
    )
    summed = lax.psum_scatter(
        (attended + downward).astype(bf16), "head", scatter_dimension=1, tiled=True
    ).astype(f32)
    hidden_out = (hidden_in.astype(f32) + summed + down_bias).astype(bf16)
    shape = (batch_size, GROUP, local_width)
    return hidden_out, new_key.reshape(shape), new_value.reshape(shape)


def solution(mesh):
    small = mesh.shape["req"] == 8 and mesh.shape["head"] == 4
    placed = (
        P("req", "head"),
        P(),
        P(),
        P(None, None, "head"),
        P("head", None),
        P("req", "head"),
        P("head"),
        P("head", "req"),
        P("head"),
        P("req", None, "head"),
        P("req", None, "head"),
        P("req"),
    )
    return jax.shard_map(
        body_small if small else body_any,
        mesh=mesh,
        in_specs=placed,
        out_specs=(P("req", "head"), P("req", None, "head"), P("req", None, "head")),
        check_vma=False,
    )
```

```python
import functools

import jax
import jax.numpy as jnp
from jax import lax
from jax.experimental import pallas as pl
from jax.experimental.pallas import tpu as pltpu
from jax.sharding import PartitionSpec as P

HD = 256
ROT = 64
GROUP = 128
BLOCK = 128
LANES = 128


epsilon = 1e-05
very_low = -1e30
f32 = jnp.float32
bf16 = jnp.bfloat16


def params(mib):
    return pltpu.CompilerParams(vmem_limit_bytes=mib * 1024 * 1024)


def cost():
    return pl.CostEstimate(flops=1024, bytes_accessed=1024, transcendentals=0)


def norm_kernel(count, split, order_ref, *refs):
    *pieces, affine_ref, out_ref = refs[: len(refs) - split]
    sent = refs[len(refs) - split :]
    total = out_ref.shape[1]
    width = total // count
    floats = [
        piece[:, start : start + width].astype(f32)
        for piece in pieces
        for start in range(0, piece.shape[1], width)
    ]
    mean = sum(jnp.sum(part, axis=-1, keepdims=True) for part in floats) / total
    floats = [part - mean for part in floats]
    spread = sum(jnp.sum(part * part, axis=-1, keepdims=True) for part in floats) / total
    inverse = lax.rsqrt(spread + epsilon)
    for k, part in enumerate(floats):
        columns = pl.ds(pl.multiple_of(order_ref[k] * width, width), width)
        out_ref[:, columns] = (
            part * inverse * affine_ref[:1, columns] + affine_ref[1:, columns]
        ).astype(bf16)
    if split:
        half = total // 2
        sent[0][...] = out_ref[:, pl.ds(pl.multiple_of(order_ref[count] * half, half), half)]


def norm_call(order, count, pieces, affine, split=False):
    rows = pieces[0].shape[0]
    total = affine.shape[1]
    block = 64
    widths = [total] + [total // 2] * split
    return pl.pallas_call(
        functools.partial(norm_kernel, count, split),
        grid_spec=pltpu.PrefetchScalarGridSpec(
            num_scalar_prefetch=1,
            grid=(rows // block,),
            in_specs=[pl.BlockSpec((block, p.shape[1]), lambda i, order: (i, 0)) for p in pieces]
            + [pl.BlockSpec((2, total), lambda i, order: (0, 0))],
            out_specs=[pl.BlockSpec((block, each), lambda i, order: (i, 0)) for each in widths],
        ),
        out_shape=[jax.ShapeDtypeStruct((rows, each), bf16) for each in widths],
        compiler_params=params(24),
        cost_estimate=cost(),
        name="layer_norm",
    )(order, *pieces, affine)


def project_kernel(heads, x_ref, w_ref, a_ref, b_ref, c_ref, q_ref, k_ref, v_ref):
    step = pl.program_id(0)
    found = jnp.dot(x_ref[...], w_ref[0], preferred_element_type=f32)

    def rotate(out_ref):
        first = found[:, :LANES]
        after = pltpu.roll(first, LANES - 1, 1)
        before = pltpu.roll(first, 1, 1)
        turned = first * a_ref[...] + after * b_ref[...] + before * c_ref[...]
        out_ref[:, :LANES] = turned.astype(bf16)
        out_ref[:, LANES:] = found[:, LANES:].astype(bf16)

    @pl.when(step < heads)
    def _():
        rotate(q_ref)

    @pl.when((step >= heads) & (step < 2 * heads))
    def _():
        rotate(k_ref)

    @pl.when(step >= 2 * heads)
    def _():
        v_ref[...] = found.astype(bf16)


def project_call(normed, weight, positions):
    rows, depth = normed.shape
    local = weight.shape[2]
    heads = local // HD
    lane = jnp.arange(LANES)
    rate = 10000.0 ** (-((lane // 2).astype(f32) * 2.0) / ROT)
    angles = positions.astype(f32)[:, None] * rate
    turns = lane < ROT
    cosine = jnp.where(turns, jnp.cos(angles), 1.0)
    sine = jnp.where(turns, jnp.sin(angles), 0.0)
    even = lane % 2 == 0
    table = pl.BlockSpec((rows, LANES), lambda j: (0, 0))
    out = jax.ShapeDtypeStruct((rows, local), bf16)
    return pl.pallas_call(
        functools.partial(project_kernel, heads),
        grid=(3 * heads,),
        in_specs=[
            pl.BlockSpec((rows, depth), lambda j: (0, 0)),
            pl.BlockSpec((1, depth, HD), lambda j: (j // heads, 0, j % heads)),
            table,
            table,
            table,
        ],
        out_specs=[
            pl.BlockSpec((rows, HD), lambda j: (0, jnp.clip(j, 0, heads - 1))),
            pl.BlockSpec((rows, HD), lambda j: (0, jnp.clip(j - heads, 0, heads - 1))),
            pl.BlockSpec((rows, HD), lambda j: (0, jnp.clip(j - 2 * heads, 0, heads - 1))),
        ],
        out_shape=[out, out, out],
        compiler_params=params(45),
        cost_estimate=cost(),
        name="projections",
    )(normed, weight, cosine, jnp.where(even, -sine, 0.0), jnp.where(even, 0.0, sine))


def attend_kernel(heads, len_ref, q_ref, kn_ref, vn_ref, kc_ref, vc_ref, out_ref):
    length = len_ref[pl.program_id(0)]
    slots = kc_ref.shape[1]
    contract = (((1,), (1,)), ((), ()))
    scale = HD ** (-0.5)
    filled = lax.broadcasted_iota(jnp.int32, (GROUP, slots), 1) < length
    causal = lax.broadcasted_iota(jnp.int32, (GROUP, GROUP), 0) >= lax.broadcasted_iota(
        jnp.int32, (GROUP, GROUP), 1
    )
    for head in range(heads):
        columns = slice(head * HD, (head + 1) * HD)
        query = q_ref[:, columns]
        old = lax.dot_general(query, kc_ref[0, :, columns], contract, preferred_element_type=f32)
        new = lax.dot_general(query, kn_ref[:, columns], contract, preferred_element_type=f32)
        old = jnp.where(filled, old * scale, very_low)
        new = jnp.where(causal, new * scale, very_low)
        top = jnp.maximum(
            jnp.max(old, axis=-1, keepdims=True), jnp.max(new, axis=-1, keepdims=True)
        )
        old = jnp.exp(old - top)
        new = jnp.exp(new - top)
        total = jnp.sum(old, axis=-1, keepdims=True) + jnp.sum(new, axis=-1, keepdims=True)
        weighted = jnp.dot(
            old.astype(bf16), vc_ref[0, :, columns], preferred_element_type=f32
        ) + jnp.dot(new.astype(bf16), vn_ref[:, columns], preferred_element_type=f32)
        out_ref[:, columns] = (weighted / total).astype(bf16)


def attend_call(lengths, query, new_key, new_value, key_cache, value_cache):
    requests, slots, local = key_cache.shape
    fresh = pl.BlockSpec((GROUP, local), lambda r, lengths: (r, 0))
    cached = pl.BlockSpec((1, slots, local), lambda r, lengths: (r, 0, 0))
    return pl.pallas_call(
        functools.partial(attend_kernel, local // HD),
        grid_spec=pltpu.PrefetchScalarGridSpec(
            num_scalar_prefetch=1,
            grid=(requests,),
            in_specs=[fresh, fresh, fresh, cached, cached],
            out_specs=fresh,
        ),
        out_shape=jax.ShapeDtypeStruct((requests * GROUP, local), bf16),
        compiler_params=params(28),
        cost_estimate=cost(),
        name="attention",
    )(lengths, query, new_key, new_value, key_cache, value_cache)


def up_kernel(depths, spots_ref, x_ref, *refs):
    weights, (bias_ref, out_ref) = refs[: len(depths)], refs[len(depths) :]
    total = bias_ref[...] + jnp.zeros(out_ref.shape, f32)
    for k, depth in enumerate(depths):
        columns = pl.ds(pl.multiple_of(spots_ref[k] * LANES, LANES), depth)
        total += jnp.dot(x_ref[:, columns], weights[k][...], preferred_element_type=f32)
    out_ref[...] = jax.nn.gelu(total, approximate=True).astype(bf16)


def up_call(spots, normed, weights, bias):
    rows, depth = normed.shape
    width = weights[0].shape[1]
    depths = [weight.shape[0] for weight in weights]
    block = 256
    return pl.pallas_call(
        functools.partial(up_kernel, depths),
        grid_spec=pltpu.PrefetchScalarGridSpec(
            num_scalar_prefetch=1,
            grid=(width // block,),
            in_specs=[pl.BlockSpec((rows, depth), lambda n, spots: (0, 0))]
            + [pl.BlockSpec((part, block), lambda n, spots: (0, n)) for part in depths]
            + [pl.BlockSpec((1, block), lambda n, spots: (0, n))],
            out_specs=pl.BlockSpec((rows, block), lambda n, spots: (0, n)),
        ),
        out_shape=jax.ShapeDtypeStruct((rows, width), bf16),
        compiler_params=params(40),
        cost_estimate=cost(),
        name="up_and_gelu",
    )(spots, normed, *weights, bias[None])


def up_half_kernel(spots_ref, rows_ref, w0, w1, w2, w3, out_ref, sum_ref):
    step = pl.program_id(0)
    steps = pl.num_programs(0)
    part = w0.shape[0]
    total = None
    for k, weight in enumerate((w0, w1, w2, w3)):
        columns = pl.ds(pl.multiple_of((spots_ref[k] * steps + step) * part, part), part)
        found = jnp.dot(rows_ref[:, columns], weight[...], preferred_element_type=f32)
        total = found if total is None else total + found

    @pl.when(step == 0)
    def _():
        sum_ref[...] = total

    @pl.when(step == steps - 1)
    def _():
        out_ref[...] = (sum_ref[...] + total).astype(out_ref.dtype)


def up_half_call(spots, x, weights, start, stop, dtype):
    rows = x.shape[0]
    width = stop - start
    steps = 2
    part = weights[0].shape[0] // steps
    column = start // width
    in_specs = [pl.BlockSpec(x.shape, lambda s, spots: (0, 0))]
    in_specs += [pl.BlockSpec((part, width), lambda s, spots: (s, column))] * 4
    return pl.pallas_call(
        up_half_kernel,
        grid_spec=pltpu.PrefetchScalarGridSpec(
            num_scalar_prefetch=1,
            grid=(steps,),
            in_specs=in_specs,
            out_specs=pl.BlockSpec((rows, width), lambda s, spots: (0, 0)),
            scratch_shapes=[pltpu.VMEM((rows, width), f32)],
        ),
        out_shape=jax.ShapeDtypeStruct((rows, width), dtype),
        compiler_params=params(28),
        cost_estimate=cost(),
        name="up_half",
    )(spots, x, *weights)


def up_rest_kernel(spots_ref, rows_ref, w0, w1, w2, w3, out_ref):
    depth = w0.shape[0]
    total = None
    for k, weight in enumerate((w0, w1, w2, w3)):
        columns = pl.ds(pl.multiple_of(spots_ref[k] * depth, depth), depth)
        part = jnp.dot(rows_ref[:, columns], weight[...], preferred_element_type=f32)
        total = part if total is None else total + part
    out_ref[...] = total.astype(out_ref.dtype)


def up_rest_call(spots, x, weights, start, stop, dtype):
    rows = x.shape[0]
    width = stop - start
    block = 256
    steps = width // block
    first = start // block
    in_specs = [pl.BlockSpec(x.shape, lambda n, spots: (0, 0))] + [
        pl.BlockSpec((w.shape[0], block), lambda n, spots: (0, first + n)) for w in weights
    ]
    return pl.pallas_call(
        up_rest_kernel,
        grid_spec=pltpu.PrefetchScalarGridSpec(
            num_scalar_prefetch=1,
            grid=(steps,),
            in_specs=in_specs,
            out_specs=pl.BlockSpec((rows, block), lambda n, spots: (0, n)),
        ),
        out_shape=jax.ShapeDtypeStruct((rows, width), dtype),
        compiler_params=params(28),
        cost_estimate=cost(),
        name="up_rest",
    )(spots, x, *weights)


def gelu_kernel(keep_ref, bias_ref, *refs):
    came, out_ref = refs[:-1], refs[-1]
    start = 0
    for ref in came:
        columns = slice(start, start + ref.shape[1])
        start += ref.shape[1]
        upward = keep_ref[:, columns] + ref[...].astype(f32) + bias_ref[:, columns]
        out_ref[:, columns] = jax.nn.gelu(upward, approximate=True).astype(bf16)


def gelu_call(keep, came, bias):
    rows, width = keep.shape
    block = 64
    whole = pl.BlockSpec((block, width), lambda i: (i, 0))
    return pl.pallas_call(
        gelu_kernel,
        grid=(rows // block,),
        in_specs=[whole, pl.BlockSpec((1, width), lambda i: (0, 0))]
        + [pl.BlockSpec((block, part.shape[1]), lambda i: (i, 0)) for part in came],
        out_specs=whole,
        out_shape=jax.ShapeDtypeStruct((rows, width), bf16),
        compiler_params=params(12),
        cost_estimate=cost(),
        name="gelu",
    )(keep, bias[None], *came)


def down_kernel(place_ref, a0, a1, c0, c1, v0, v1, v2, v3, o0, o1, o2, o3, own_ref, hold_ref, send_ref, total):
    step = pl.program_id(0)
    steps = pl.num_programs(0)
    rows, width = a0.shape[0], v0.shape[1]

    weight = jnp.concatenate([v0[...], v1[...], v2[...], v3[...]], axis=1)
    active = jnp.concatenate([a0[...], a1[...]], axis=0)
    part = jnp.dot(active, weight, preferred_element_type=f32)

    @pl.when(step == 0)
    def _():
        out_weight = jnp.concatenate([o0[...], o1[...], o2[...], o3[...]], axis=1)
        context = jnp.concatenate([c0[...], c1[...]], axis=0)
        total[...] = part + jnp.dot(context, out_weight, preferred_element_type=f32)

    @pl.when((step > 0) & (step < steps - 1))
    def _():
        total[...] += part

    @pl.when(step == steps - 1)
    def _():
        for k in range(4):
            columns = slice(k * width, (k + 1) * width)
            found = total[:, columns] + part[:, columns]

            @pl.when(place_ref[4 + k] == 0)
            def _():
                own_ref[...] = found

            @pl.when(place_ref[4 + k] == 1)
            def _():
                send_ref[: 2 * rows] = found.astype(bf16)

            @pl.when(place_ref[4 + k] == 2)
            def _():
                hold_ref[...] = found

            @pl.when(place_ref[4 + k] == 3)
            def _():
                send_ref[2 * rows :] = found.astype(bf16)


def down_call(place, active, context, weights, out_weight, start, width):
    rows, depth = active[0].shape
    local = context[0].shape[1]
    steps = 2
    part = depth // steps
    per = out_weight.shape[1] // 8 // width
    in_specs = [pl.BlockSpec((rows, part), lambda s, place: (0, s))] * 2
    in_specs += [pl.BlockSpec((rows, local), lambda s, place: (0, 0))] * 2
    for _, column in weights:
        in_specs.append(pl.BlockSpec((part, width), lambda s, place, column=column: (s, column)))
    for k in range(4):
        in_specs.append(
            pl.BlockSpec(
                (local, width), lambda s, place, k=k: (0, place[k] * per + start // width)
            )
        )
    result = pl.BlockSpec((2 * rows, width), lambda s, place: (0, 0))
    double = pl.BlockSpec((4 * rows, width), lambda s, place: (0, 0))
    return pl.pallas_call(
        down_kernel,
        grid_spec=pltpu.PrefetchScalarGridSpec(
            num_scalar_prefetch=1,
            grid=(steps,),
            in_specs=in_specs,
            out_specs=[result, result, double],
            scratch_shapes=[pltpu.VMEM((2 * rows, 4 * width), f32)],
        ),
        out_shape=[jax.ShapeDtypeStruct((2 * rows, width), f32)] * 2
        + [jax.ShapeDtypeStruct((4 * rows, width), bf16)],
        compiler_params=params(24),
        cost_estimate=cost(),
        name="down_and_output",
    )(place, *active, *context, *[w for w, _ in weights], *[out_weight] * 4)


def sum_kernel(own_ref, hold_ref, came_ref, kept_ref, send_ref):
    rows = own_ref.shape[0]
    kept_ref[...] = own_ref[...] + came_ref[:rows].astype(f32)
    send_ref[...] = (hold_ref[...] + came_ref[rows:].astype(f32)).astype(bf16)


def sum_call(own, hold, came):
    return pl.pallas_call(
        sum_kernel,
        out_shape=[
            jax.ShapeDtypeStruct(own.shape, f32),
            jax.ShapeDtypeStruct(own.shape, bf16),
        ],
        compiler_params=params(12),
        cost_estimate=cost(),
        name="sum_near",
    )(own, hold, came)


def join_kernel(widths, *refs):
    keep_ref, send_ref = refs[-2:]
    rows = keep_ref.shape[0]
    start = 0
    for piece, width in enumerate(widths):
        summed = refs[2 * piece][...] + refs[2 * piece + 1][...].astype(f32)
        keep_ref[:, start : start + width] = summed[:rows]
        send_ref[:, start : start + width] = summed[rows:]
        start += width


def join_call(pieces):
    widths = [piece[0].shape[1] for piece in pieces]
    rows = pieces[0][0].shape[0] // 2
    out = jax.ShapeDtypeStruct((rows, sum(widths)), f32)
    return pl.pallas_call(
        functools.partial(join_kernel, widths),
        out_shape=[out, out],
        compiler_params=params(12),
        cost_estimate=cost(),
        name="sum_far",
    )(*[array for piece in pieces for array in piece])


def close_kernel(side_ref, hidden_ref, bias_ref, own_ref, other_ref, out_ref):
    width = own_ref.shape[1]
    for source, side in ((own_ref, side_ref[0]), (other_ref, 1 - side_ref[0])):
        columns = pl.ds(pl.multiple_of(side * width, width), width)
        out_ref[:, columns] = (
            hidden_ref[:, columns].astype(f32) + source[...] + bias_ref[:, columns]
        ).astype(bf16)


def close_call(side, hidden, bias, own, other):
    return pl.pallas_call(
        close_kernel,
        in_specs=[pl.BlockSpec(memory_space=pltpu.SMEM)]
        + [pl.BlockSpec(memory_space=pltpu.VMEM)] * 4,
        out_shape=jax.ShapeDtypeStruct(hidden.shape, bf16),
        compiler_params=params(12),
        cost_estimate=cost(),
        name="final_sum",
    )(side, hidden, bias[None], own, other)


CORE, X, Y = 1, 2, 4


def swap(value, axis, size, mask):
    return lax.ppermute(value, axis, [(i, i ^ mask) for i in range(size)])


def after(value, earlier):
    return lax.optimization_barrier((value, earlier))[0]


def body_small(
    hidden_in,
    norm_gain,
    norm_shift,
    attend_weight,
    output_weight,
    up_weight,
    up_bias,
    down_weight,
    down_bias,
    key_cache,
    value_cache,
    cached_len,
):
    over_req = functools.partial(swap, axis="req", size=8)
    over_head = functools.partial(swap, axis="head", size=4)
    me = lax.axis_index("req").astype(jnp.int32)
    line = lax.axis_index("head").astype(jnp.int32)
    side = me & 1
    chips = jnp.arange(4, dtype=jnp.int32)
    batch_size = key_cache.shape[0]
    local_width = output_weight.shape[0]

    far = over_head(hidden_in, mask=2)
    near = over_head(hidden_in, mask=1)
    up_x = over_req(up_weight, mask=X)
    down_y = over_req(down_weight, mask=Y)
    up_core = over_req(up_weight, mask=CORE)
    last = over_head(far, mask=1)
    pair = jnp.concatenate([hidden_in, near], axis=1)
    affine = jnp.stack([norm_gain, norm_shift])
    quarter = down_weight.shape[1] // 4
    mine = [down_weight[:, k * quarter : (k + 1) * quarter] for k in range(4)]
    last, pair, affine, mine = lax.optimization_barrier((last, pair, affine, mine))

    order = jnp.concatenate([line ^ chips, (1 - (me >> 2))[None]])
    normed, for_other = norm_call(order, 4, [pair, far, last], affine, split=True)
    normed_other = over_req(for_other, mask=Y)
    up_x, up_core, normed_next = lax.optimization_barrier((up_x, up_core, normed))
    up_x_core = over_req(up_x, mask=CORE)
    down_x = over_req(after(down_weight, up_x), mask=X)
    down_y, normed_next = lax.optimization_barrier((down_y, normed_next))

    half = down_weight.shape[1] // 2
    forward_y = [down_y[:, k * quarter : (k + 1) * quarter] for k in range(2)]
    diagonal = [over_req(forward_y[0], mask=X)]
    normed_next, forward_y = lax.optimization_barrier((normed_next, forward_y))

    positions = (cached_len[:, None] + jnp.arange(GROUP, dtype=jnp.int32)[None, :]).reshape(-1)
    query, new_key, new_value = project_call(
        normed_next, attend_weight.transpose(1, 0, 2), positions
    )

    blocks = me ^ jnp.array([0, X, CORE, X | CORE], jnp.int32)
    weights = [up_weight, up_x, up_core, up_x_core]
    units = up_weight.shape[1]
    keep = up_half_call(blocks, after(normed, query), weights, 0, units, f32)
    other = after(normed_other, keep)
    came = []
    cut = units * 5 // 8
    for call, start, stop in ((up_half_call, 0, cut), (up_rest_call, cut, units)):
        send = call(blocks & 3, other, weights, start, stop, bf16)
        came.append(over_req(send, mask=Y))
        other = after(other, send)

    query = after(query, send)
    context = attend_call(cached_len, query, new_key, new_value, key_cache, value_cache)
    context_other = over_req(context, mask=CORE)

    came, context_other = lax.optimization_barrier((came, context_other))
    diagonal.append(over_req(after(forward_y[1], diagonal[0]), mask=X))
    forward_x = [down_x[:, half + k * quarter : half + (k + 1) * quarter] for k in range(2)]
    forward_x = after(forward_x, came)
    diagonal += [over_req(part, mask=Y) for part in forward_x]

    active = gelu_call(keep, came, up_bias)
    active_other = over_req(after(active, diagonal[0]), mask=CORE)

    blocks = me ^ (2 * chips)
    place = jnp.concatenate([blocks, line ^ (blocks >> 1)])
    results, near_sums, far_sums = [], [], []
    rows = active, active_other
    for k in range(4):
        if k >= 2:
            rows = after(rows, near_sums[k - 2])
        if k == 3:
            rows = after(rows, far_sums[0])
        own, hold, send = down_call(
            place,
            rows,
            (context, context_other),
            [
                (mine[k], 0),
                (down_x, k) if k < 2 else (forward_x[k - 2], 0),
                (forward_y[k], 0) if k < 2 else (down_y, k),
                (diagonal[k], 0),
            ],
            output_weight,
            k * quarter,
            quarter,
        )
        rows = after(rows, send)
        came = over_head(send, mask=1)
        if k:
            came = after(came, far_sums[-1])
        own, second = sum_call(own, hold, came)
        near_sums.append(second)
        far_sums.append(over_head(second, mask=2))
        results.append((own, far_sums[-1]))
    own, send = join_call(results)
    other = over_req(send, mask=CORE)
    hidden_out = close_call(side[None], hidden_in, down_bias, own, other)
    shape = (batch_size, GROUP, local_width)
    return hidden_out, new_key.reshape(shape), new_value.reshape(shape)


def body_any(
    hidden_in,
    norm_gain,
    norm_shift,
    attend_weight,
    output_weight,
    up_weight,
    up_bias,
    down_weight,
    down_bias,
    key_cache,
    value_cache,
    cached_len,
):
    batch_size = key_cache.shape[0]
    local_width = output_weight.shape[0]
    gathered = lax.all_gather(hidden_in, "head", axis=1, tiled=True)
    affine = jnp.stack([norm_gain, norm_shift])
    (normed,) = norm_call(jnp.zeros((1,), jnp.int32), 1, [gathered], affine)
    positions = (cached_len[:, None] + jnp.arange(GROUP, dtype=jnp.int32)[None, :]).reshape(-1)
    query, new_key, new_value = project_call(
        normed, attend_weight.transpose(1, 0, 2), positions
    )
    context = attend_call(cached_len, query, new_key, new_value, key_cache, value_cache)
    attended = jnp.dot(context, output_weight, preferred_element_type=f32)
    up_whole = lax.all_gather(up_weight, "req", axis=0, tiled=True)
    active = up_call(jnp.zeros((1,), jnp.int32), normed, [up_whole], up_bias)
    downward = jnp.dot(
        active,
        lax.all_gather(down_weight, "req", axis=1, tiled=True),
        preferred_element_type=f32,
    )
    summed = lax.psum_scatter(
        (attended + downward).astype(bf16), "head", scatter_dimension=1, tiled=True
    ).astype(f32)
    hidden_out = (hidden_in.astype(f32) + summed + down_bias).astype(bf16)
    shape = (batch_size, GROUP, local_width)
    return hidden_out, new_key.reshape(shape), new_value.reshape(shape)


def solution(mesh):
    small = mesh.shape["req"] == 8 and mesh.shape["head"] == 4
    placed = (
        P("req", "head"),
        P(),
        P(),
        P(None, None, "head"),
        P("head", None),
        P("req", "head"),
        P("head"),
        P("head", "req"),
        P("head"),
        P("req", None, "head"),
        P("req", None, "head"),
        P("req"),
    )
    return jax.shard_map(
        body_small if small else body_any,
        mesh=mesh,
        in_specs=placed,
        out_specs=(P("req", "head"), P("req", None, "head"), P("req", None, "head")),
        check_vma=False,
    )
```

```python
import functools

import jax
import jax.numpy as jnp
from jax import lax
from jax.experimental import pallas as pl
from jax.experimental.pallas import tpu as pltpu
from jax.sharding import PartitionSpec as P

HD = 256
ROT = 64
GROUP = 128
BLOCK = 128
LANES = 128


epsilon = 1e-05
very_low = -1e30
f32 = jnp.float32
bf16 = jnp.bfloat16


def params(mib):
    return pltpu.CompilerParams(vmem_limit_bytes=mib * 1024 * 1024)


def cost():
    return pl.CostEstimate(flops=1024, bytes_accessed=1024, transcendentals=0)


def norm_kernel(count, split, order_ref, *refs):
    *pieces, affine_ref, out_ref = refs[: len(refs) - split]
    sent = refs[len(refs) - split :]
    total = out_ref.shape[1]
    width = total // count
    floats = [
        piece[:, start : start + width].astype(f32)
        for piece in pieces
        for start in range(0, piece.shape[1], width)
    ]
    mean = sum(jnp.sum(part, axis=-1, keepdims=True) for part in floats) / total
    floats = [part - mean for part in floats]
    spread = sum(jnp.sum(part * part, axis=-1, keepdims=True) for part in floats) / total
    inverse = lax.rsqrt(spread + epsilon)
    for k, part in enumerate(floats):
        columns = pl.ds(pl.multiple_of(order_ref[k] * width, width), width)
        out_ref[:, columns] = (
            part * inverse * affine_ref[:1, columns] + affine_ref[1:, columns]
        ).astype(bf16)
    if split:
        half = total // 2
        sent[0][...] = out_ref[:, pl.ds(pl.multiple_of(order_ref[count] * half, half), half)]


def norm_call(order, count, pieces, affine, split=False):
    rows = pieces[0].shape[0]
    total = affine.shape[1]
    block = 64
    widths = [total] + [total // 2] * split
    return pl.pallas_call(
        functools.partial(norm_kernel, count, split),
        grid_spec=pltpu.PrefetchScalarGridSpec(
            num_scalar_prefetch=1,
            grid=(rows // block,),
            in_specs=[pl.BlockSpec((block, p.shape[1]), lambda i, order: (i, 0)) for p in pieces]
            + [pl.BlockSpec((2, total), lambda i, order: (0, 0))],
            out_specs=[pl.BlockSpec((block, each), lambda i, order: (i, 0)) for each in widths],
        ),
        out_shape=[jax.ShapeDtypeStruct((rows, each), bf16) for each in widths],
        compiler_params=params(24),
        cost_estimate=cost(),
        name="layer_norm",
    )(order, *pieces, affine)


def project_kernel(heads, x_ref, w_ref, a_ref, b_ref, c_ref, q_ref, k_ref, v_ref):
    step = pl.program_id(0)
    found = jnp.dot(x_ref[...], w_ref[0], preferred_element_type=f32)

    def rotate(out_ref):
        first = found[:, :LANES]
        after = pltpu.roll(first, LANES - 1, 1)
        before = pltpu.roll(first, 1, 1)
        turned = first * a_ref[...] + after * b_ref[...] + before * c_ref[...]
        out_ref[:, :LANES] = turned.astype(bf16)
        out_ref[:, LANES:] = found[:, LANES:].astype(bf16)

    @pl.when(step < heads)
    def _():
        rotate(q_ref)

    @pl.when((step >= heads) & (step < 2 * heads))
    def _():
        rotate(k_ref)

    @pl.when(step >= 2 * heads)
    def _():
        v_ref[...] = found.astype(bf16)


def project_call(normed, weight, positions):
    rows, depth = normed.shape
    local = weight.shape[2]
    heads = local // HD
    lane = jnp.arange(LANES)
    rate = 10000.0 ** (-((lane // 2).astype(f32) * 2.0) / ROT)
    angles = positions.astype(f32)[:, None] * rate
    turns = lane < ROT
    cosine = jnp.where(turns, jnp.cos(angles), 1.0)
    sine = jnp.where(turns, jnp.sin(angles), 0.0)
    even = lane % 2 == 0
    table = pl.BlockSpec((rows, LANES), lambda j: (0, 0))
    out = jax.ShapeDtypeStruct((rows, local), bf16)
    return pl.pallas_call(
        functools.partial(project_kernel, heads),
        grid=(3 * heads,),
        in_specs=[
            pl.BlockSpec((rows, depth), lambda j: (0, 0)),
            pl.BlockSpec((1, depth, HD), lambda j: (j // heads, 0, j % heads)),
            table,
            table,
            table,
        ],
        out_specs=[
            pl.BlockSpec((rows, HD), lambda j: (0, jnp.clip(j, 0, heads - 1))),
            pl.BlockSpec((rows, HD), lambda j: (0, jnp.clip(j - heads, 0, heads - 1))),
            pl.BlockSpec((rows, HD), lambda j: (0, jnp.clip(j - 2 * heads, 0, heads - 1))),
        ],
        out_shape=[out, out, out],
        compiler_params=params(45),
        cost_estimate=cost(),
        name="projections",
    )(normed, weight, cosine, jnp.where(even, -sine, 0.0), jnp.where(even, 0.0, sine))


def attend_kernel(heads, len_ref, q_ref, kn_ref, vn_ref, kc_ref, vc_ref, out_ref):
    length = len_ref[pl.program_id(0)]
    slots = kc_ref.shape[1]
    contract = (((1,), (1,)), ((), ()))
    scale = HD ** (-0.5)
    filled = lax.broadcasted_iota(jnp.int32, (GROUP, slots), 1) < length
    causal = lax.broadcasted_iota(jnp.int32, (GROUP, GROUP), 0) >= lax.broadcasted_iota(
        jnp.int32, (GROUP, GROUP), 1
    )
    for head in range(heads):
        columns = slice(head * HD, (head + 1) * HD)
        query = q_ref[:, columns]
        old = lax.dot_general(query, kc_ref[0, :, columns], contract, preferred_element_type=f32)
        new = lax.dot_general(query, kn_ref[:, columns], contract, preferred_element_type=f32)
        old = jnp.where(filled, old * scale, very_low)
        new = jnp.where(causal, new * scale, very_low)
        top = jnp.maximum(
            jnp.max(old, axis=-1, keepdims=True), jnp.max(new, axis=-1, keepdims=True)
        )
        old = jnp.exp(old - top)
        new = jnp.exp(new - top)
        total = jnp.sum(old, axis=-1, keepdims=True) + jnp.sum(new, axis=-1, keepdims=True)
        weighted = jnp.dot(
            old.astype(bf16), vc_ref[0, :, columns], preferred_element_type=f32
        ) + jnp.dot(new.astype(bf16), vn_ref[:, columns], preferred_element_type=f32)
        out_ref[:, columns] = (weighted / total).astype(bf16)


def attend_call(lengths, query, new_key, new_value, key_cache, value_cache):
    requests, slots, local = key_cache.shape
    fresh = pl.BlockSpec((GROUP, local), lambda r, lengths: (r, 0))
    cached = pl.BlockSpec((1, slots, local), lambda r, lengths: (r, 0, 0))
    return pl.pallas_call(
        functools.partial(attend_kernel, local // HD),
        grid_spec=pltpu.PrefetchScalarGridSpec(
            num_scalar_prefetch=1,
            grid=(requests,),
            in_specs=[fresh, fresh, fresh, cached, cached],
            out_specs=fresh,
        ),
        out_shape=jax.ShapeDtypeStruct((requests * GROUP, local), bf16),
        compiler_params=params(28),
        cost_estimate=cost(),
        name="attention",
    )(lengths, query, new_key, new_value, key_cache, value_cache)


def up_kernel(depths, spots_ref, x_ref, *refs):
    weights, (bias_ref, out_ref) = refs[: len(depths)], refs[len(depths) :]
    total = bias_ref[...] + jnp.zeros(out_ref.shape, f32)
    for k, depth in enumerate(depths):
        columns = pl.ds(pl.multiple_of(spots_ref[k] * LANES, LANES), depth)
        total += jnp.dot(x_ref[:, columns], weights[k][...], preferred_element_type=f32)
    out_ref[...] = jax.nn.gelu(total, approximate=True).astype(bf16)


def up_call(spots, normed, weights, bias):
    rows, depth = normed.shape
    width = weights[0].shape[1]
    depths = [weight.shape[0] for weight in weights]
    block = 256
    return pl.pallas_call(
        functools.partial(up_kernel, depths),
        grid_spec=pltpu.PrefetchScalarGridSpec(
            num_scalar_prefetch=1,
            grid=(width // block,),
            in_specs=[pl.BlockSpec((rows, depth), lambda n, spots: (0, 0))]
            + [pl.BlockSpec((part, block), lambda n, spots: (0, n)) for part in depths]
            + [pl.BlockSpec((1, block), lambda n, spots: (0, n))],
            out_specs=pl.BlockSpec((rows, block), lambda n, spots: (0, n)),
        ),
        out_shape=jax.ShapeDtypeStruct((rows, width), bf16),
        compiler_params=params(40),
        cost_estimate=cost(),
        name="up_and_gelu",
    )(spots, normed, *weights, bias[None])


def up_half_kernel(spots_ref, rows_ref, w0, w1, w2, w3, out_ref, sum_ref):
    step = pl.program_id(0)
    steps = pl.num_programs(0)
    part = w0.shape[0]
    total = None
    for k, weight in enumerate((w0, w1, w2, w3)):
        columns = pl.ds(pl.multiple_of((spots_ref[k] * steps + step) * part, part), part)
        found = jnp.dot(rows_ref[:, columns], weight[...], preferred_element_type=f32)
        total = found if total is None else total + found

    @pl.when(step == 0)
    def _():
        sum_ref[...] = total

    @pl.when(step == steps - 1)
    def _():
        out_ref[...] = (sum_ref[...] + total).astype(out_ref.dtype)


def up_half_call(spots, x, weights, start, stop, dtype):
    rows = x.shape[0]
    width = stop - start
    steps = 2
    part = weights[0].shape[0] // steps
    column = start // width
    in_specs = [pl.BlockSpec(x.shape, lambda s, spots: (0, 0))]
    in_specs += [pl.BlockSpec((part, width), lambda s, spots: (s, column))] * 4
    return pl.pallas_call(
        up_half_kernel,
        grid_spec=pltpu.PrefetchScalarGridSpec(
            num_scalar_prefetch=1,
            grid=(steps,),
            in_specs=in_specs,
            out_specs=pl.BlockSpec((rows, width), lambda s, spots: (0, 0)),
            scratch_shapes=[pltpu.VMEM((rows, width), f32)],
        ),
        out_shape=jax.ShapeDtypeStruct((rows, width), dtype),
        compiler_params=params(28),
        cost_estimate=cost(),
        name="up_half",
    )(spots, x, *weights)


def up_rest_kernel(spots_ref, rows_ref, w0, w1, w2, w3, out_ref):
    depth = w0.shape[0]
    total = None
    for k, weight in enumerate((w0, w1, w2, w3)):
        columns = pl.ds(pl.multiple_of(spots_ref[k] * depth, depth), depth)
        part = jnp.dot(rows_ref[:, columns], weight[...], preferred_element_type=f32)
        total = part if total is None else total + part
    out_ref[...] = total.astype(out_ref.dtype)


def up_rest_call(spots, x, weights, start, stop, dtype):
    rows = x.shape[0]
    width = stop - start
    block = 256
    steps = width // block
    first = start // block
    in_specs = [pl.BlockSpec(x.shape, lambda n, spots: (0, 0))] + [
        pl.BlockSpec((w.shape[0], block), lambda n, spots: (0, first + n)) for w in weights
    ]
    return pl.pallas_call(
        up_rest_kernel,
        grid_spec=pltpu.PrefetchScalarGridSpec(
            num_scalar_prefetch=1,
            grid=(steps,),
            in_specs=in_specs,
            out_specs=pl.BlockSpec((rows, block), lambda n, spots: (0, n)),
        ),
        out_shape=jax.ShapeDtypeStruct((rows, width), dtype),
        compiler_params=params(28),
        cost_estimate=cost(),
        name="up_rest",
    )(spots, x, *weights)


def gelu_kernel(keep_ref, bias_ref, *refs):
    came, out_ref = refs[:-1], refs[-1]
    start = 0
    for ref in came:
        columns = slice(start, start + ref.shape[1])
        start += ref.shape[1]
        upward = keep_ref[:, columns] + ref[...].astype(f32) + bias_ref[:, columns]
        out_ref[:, columns] = jax.nn.gelu(upward, approximate=True).astype(bf16)


def gelu_call(keep, came, bias):
    rows, width = keep.shape
    block = 64
    whole = pl.BlockSpec((block, width), lambda i: (i, 0))
    return pl.pallas_call(
        gelu_kernel,
        grid=(rows // block,),
        in_specs=[whole, pl.BlockSpec((1, width), lambda i: (0, 0))]
        + [pl.BlockSpec((block, part.shape[1]), lambda i: (i, 0)) for part in came],
        out_specs=whole,
        out_shape=jax.ShapeDtypeStruct((rows, width), bf16),
        compiler_params=params(12),
        cost_estimate=cost(),
        name="gelu",
    )(keep, bias[None], *came)


def down_kernel(place_ref, a0, a1, c0, c1, v0, v1, v2, v3, o0, o1, o2, o3, own_ref, hold_ref, send_ref, total):
    step = pl.program_id(0)
    steps = pl.num_programs(0)
    rows, width = a0.shape[0], v0.shape[1]

    weight = jnp.concatenate([v0[...], v1[...], v2[...], v3[...]], axis=1)
    active = jnp.concatenate([a0[...], a1[...]], axis=0)
    part = jnp.dot(active, weight, preferred_element_type=f32)

    @pl.when(step == 0)
    def _():
        out_weight = jnp.concatenate([o0[...], o1[...], o2[...], o3[...]], axis=1)
        context = jnp.concatenate([c0[...], c1[...]], axis=0)
        total[...] = part + jnp.dot(context, out_weight, preferred_element_type=f32)

    @pl.when((step > 0) & (step < steps - 1))
    def _():
        total[...] += part

    @pl.when(step == steps - 1)
    def _():
        for k in range(4):
            columns = slice(k * width, (k + 1) * width)
            found = total[:, columns] + part[:, columns]

            @pl.when(place_ref[4 + k] == 0)
            def _():
                own_ref[...] = found

            @pl.when(place_ref[4 + k] == 1)
            def _():
                send_ref[: 2 * rows] = found.astype(bf16)

            @pl.when(place_ref[4 + k] == 2)
            def _():
                hold_ref[...] = found

            @pl.when(place_ref[4 + k] == 3)
            def _():
                send_ref[2 * rows :] = found.astype(bf16)


def down_call(place, active, context, weights, out_weight, start, width):
    rows, depth = active[0].shape
    local = context[0].shape[1]
    steps = 2
    part = depth // steps
    per = out_weight.shape[1] // 8 // width
    in_specs = [pl.BlockSpec((rows, part), lambda s, place: (0, s))] * 2
    in_specs += [pl.BlockSpec((rows, local), lambda s, place: (0, 0))] * 2
    for _, column in weights:
        in_specs.append(pl.BlockSpec((part, width), lambda s, place, column=column: (s, column)))
    for k in range(4):
        in_specs.append(
            pl.BlockSpec(
                (local, width), lambda s, place, k=k: (0, place[k] * per + start // width)
            )
        )
    result = pl.BlockSpec((2 * rows, width), lambda s, place: (0, 0))
    double = pl.BlockSpec((4 * rows, width), lambda s, place: (0, 0))
    return pl.pallas_call(
        down_kernel,
        grid_spec=pltpu.PrefetchScalarGridSpec(
            num_scalar_prefetch=1,
            grid=(steps,),
            in_specs=in_specs,
            out_specs=[result, result, double],
            scratch_shapes=[pltpu.VMEM((2 * rows, 4 * width), f32)],
        ),
        out_shape=[jax.ShapeDtypeStruct((2 * rows, width), f32)] * 2
        + [jax.ShapeDtypeStruct((4 * rows, width), bf16)],
        compiler_params=params(24),
        cost_estimate=cost(),
        name="down_and_output",
    )(place, *active, *context, *[w for w, _ in weights], *[out_weight] * 4)


def sum_kernel(own_ref, hold_ref, came_ref, kept_ref, send_ref):
    rows = own_ref.shape[0]
    kept_ref[...] = own_ref[...] + came_ref[:rows].astype(f32)
    send_ref[...] = (hold_ref[...] + came_ref[rows:].astype(f32)).astype(bf16)


def sum_call(own, hold, came):
    return pl.pallas_call(
        sum_kernel,
        out_shape=[
            jax.ShapeDtypeStruct(own.shape, f32),
            jax.ShapeDtypeStruct(own.shape, bf16),
        ],
        compiler_params=params(12),
        cost_estimate=cost(),
        name="sum_near",
    )(own, hold, came)


def join_kernel(widths, *refs):
    keep_ref, send_ref = refs[-2:]
    rows = keep_ref.shape[0]
    start = 0
    for piece, width in enumerate(widths):
        summed = refs[2 * piece][...] + refs[2 * piece + 1][...].astype(f32)
        keep_ref[:, start : start + width] = summed[:rows]
        send_ref[:, start : start + width] = summed[rows:]
        start += width


def join_call(pieces):
    widths = [piece[0].shape[1] for piece in pieces]
    rows = pieces[0][0].shape[0] // 2
    out = jax.ShapeDtypeStruct((rows, sum(widths)), f32)
    return pl.pallas_call(
        functools.partial(join_kernel, widths),
        out_shape=[out, out],
        compiler_params=params(12),
        cost_estimate=cost(),
        name="sum_far",
    )(*[array for piece in pieces for array in piece])


def close_kernel(side_ref, hidden_ref, bias_ref, own_ref, other_ref, out_ref):
    width = own_ref.shape[1]
    for source, side in ((own_ref, side_ref[0]), (other_ref, 1 - side_ref[0])):
        columns = pl.ds(pl.multiple_of(side * width, width), width)
        out_ref[:, columns] = (
            hidden_ref[:, columns].astype(f32) + source[...] + bias_ref[:, columns]
        ).astype(bf16)


def close_call(side, hidden, bias, own, other):
    return pl.pallas_call(
        close_kernel,
        in_specs=[pl.BlockSpec(memory_space=pltpu.SMEM)]
        + [pl.BlockSpec(memory_space=pltpu.VMEM)] * 4,
        out_shape=jax.ShapeDtypeStruct(hidden.shape, bf16),
        compiler_params=params(12),
        cost_estimate=cost(),
        name="final_sum",
    )(side, hidden, bias[None], own, other)


CORE, X, Y = 1, 2, 4


def swap(value, axis, size, mask):
    return lax.ppermute(value, axis, [(i, i ^ mask) for i in range(size)])


def after(value, earlier):
    return lax.optimization_barrier((value, earlier))[0]


def body_small(
    hidden_in,
    norm_gain,
    norm_shift,
    attend_weight,
    output_weight,
    up_weight,
    up_bias,
    down_weight,
    down_bias,
    key_cache,
    value_cache,
    cached_len,
):
    over_req = functools.partial(swap, axis="req", size=8)
    over_head = functools.partial(swap, axis="head", size=4)
    me = lax.axis_index("req").astype(jnp.int32)
    line = lax.axis_index("head").astype(jnp.int32)
    side = me & 1
    chips = jnp.arange(4, dtype=jnp.int32)
    batch_size = key_cache.shape[0]
    local_width = output_weight.shape[0]

    far = over_head(hidden_in, mask=2)
    near = over_head(hidden_in, mask=1)
    up_x = over_req(up_weight, mask=X)
    down_y = over_req(down_weight, mask=Y)
    up_core = over_req(up_weight, mask=CORE)
    last = over_head(far, mask=1)
    pair = jnp.concatenate([hidden_in, near], axis=1)
    affine = jnp.stack([norm_gain, norm_shift])
    quarter = down_weight.shape[1] // 4
    mine = [down_weight[:, k * quarter : (k + 1) * quarter] for k in range(4)]
    last, pair, affine, mine = lax.optimization_barrier((last, pair, affine, mine))

    order = jnp.concatenate([line ^ chips, (1 - (me >> 2))[None]])
    normed, for_other = norm_call(order, 4, [pair, far, last], affine, split=True)
    normed_other = over_req(for_other, mask=Y)
    up_x, up_core, normed_next = lax.optimization_barrier((up_x, up_core, normed))
    up_x_core = over_req(up_x, mask=CORE)
    down_x = over_req(after(down_weight, up_x), mask=X)
    down_y, normed_next = lax.optimization_barrier((down_y, normed_next))

    half = down_weight.shape[1] // 2
    forward_y = [down_y[:, k * quarter : (k + 1) * quarter] for k in range(2)]
    diagonal = [over_req(forward_y[0], mask=X)]
    normed_next, forward_y = lax.optimization_barrier((normed_next, forward_y))

    positions = (cached_len[:, None] + jnp.arange(GROUP, dtype=jnp.int32)[None, :]).reshape(-1)
    query, new_key, new_value = project_call(
        normed_next, attend_weight.transpose(1, 0, 2), positions
    )

    blocks = me ^ jnp.array([0, X, CORE, X | CORE], jnp.int32)
    weights = [up_weight, up_x, up_core, up_x_core]
    units = up_weight.shape[1]
    keep = up_half_call(blocks, after(normed, query), weights, 0, units, f32)
    other = after(normed_other, keep)
    came = []
    cut = units * 5 // 8
    for call, start, stop in ((up_half_call, 0, cut), (up_rest_call, cut, units)):
        send = call(blocks & 3, other, weights, start, stop, bf16)
        came.append(over_req(send, mask=Y))
        other = after(other, send)

    query = after(query, send)
    context = attend_call(cached_len, query, new_key, new_value, key_cache, value_cache)
    context_other = over_req(context, mask=CORE)

    came, context_other = lax.optimization_barrier((came, context_other))
    diagonal.append(over_req(after(forward_y[1], diagonal[0]), mask=X))
    forward_x = [down_x[:, half + k * quarter : half + (k + 1) * quarter] for k in range(2)]
    forward_x = after(forward_x, came)
    diagonal.append(over_req(forward_x[0], mask=Y))

    active = gelu_call(keep, came, up_bias)
    active_other = over_req(after(active, diagonal[0]), mask=CORE)

    blocks = me ^ (2 * chips)
    place = jnp.concatenate([blocks, line ^ (blocks >> 1)])
    results, near_sums, far_sums = [], [], []
    rows = active, active_other
    for k in range(4):
        if k >= 2:
            rows = after(rows, near_sums[k - 2])
        if k == 3:
            rows = after(rows, far_sums[0])
        own, hold, send = down_call(
            place,
            rows,
            (context, context_other),
            [
                (mine[k], 0),
                (down_x, k) if k < 2 else (forward_x[k - 2], 0),
                (forward_y[k], 0) if k < 2 else (down_y, k),
                (diagonal[k], 0),
            ],
            output_weight,
            k * quarter,
            quarter,
        )
        rows = after(rows, send)
        if k == 0:
            diagonal.append(over_req(after(forward_x[1], send), mask=Y))
        came = over_head(send, mask=1)
        if k:
            came = after(came, far_sums[-1])
        own, second = sum_call(own, hold, came)
        near_sums.append(second)
        far_sums.append(over_head(second, mask=2))
        results.append((own, far_sums[-1]))
    own, send = join_call(results)
    other = over_req(send, mask=CORE)
    hidden_out = close_call(side[None], hidden_in, down_bias, own, other)
    shape = (batch_size, GROUP, local_width)
    return hidden_out, new_key.reshape(shape), new_value.reshape(shape)


def body_any(
    hidden_in,
    norm_gain,
    norm_shift,
    attend_weight,
    output_weight,
    up_weight,
    up_bias,
    down_weight,
    down_bias,
    key_cache,
    value_cache,
    cached_len,
):
    batch_size = key_cache.shape[0]
    local_width = output_weight.shape[0]
    gathered = lax.all_gather(hidden_in, "head", axis=1, tiled=True)
    affine = jnp.stack([norm_gain, norm_shift])
    (normed,) = norm_call(jnp.zeros((1,), jnp.int32), 1, [gathered], affine)
    positions = (cached_len[:, None] + jnp.arange(GROUP, dtype=jnp.int32)[None, :]).reshape(-1)
    query, new_key, new_value = project_call(
        normed, attend_weight.transpose(1, 0, 2), positions
    )
    context = attend_call(cached_len, query, new_key, new_value, key_cache, value_cache)
    attended = jnp.dot(context, output_weight, preferred_element_type=f32)
    up_whole = lax.all_gather(up_weight, "req", axis=0, tiled=True)
    active = up_call(jnp.zeros((1,), jnp.int32), normed, [up_whole], up_bias)
    downward = jnp.dot(
        active,
        lax.all_gather(down_weight, "req", axis=1, tiled=True),
        preferred_element_type=f32,
    )
    summed = lax.psum_scatter(
        (attended + downward).astype(bf16), "head", scatter_dimension=1, tiled=True
    ).astype(f32)
    hidden_out = (hidden_in.astype(f32) + summed + down_bias).astype(bf16)
    shape = (batch_size, GROUP, local_width)
    return hidden_out, new_key.reshape(shape), new_value.reshape(shape)


def solution(mesh):
    small = mesh.shape["req"] == 8 and mesh.shape["head"] == 4
    placed = (
        P("req", "head"),
        P(),
        P(),
        P(None, None, "head"),
        P("head", None),
        P("req", "head"),
        P("head"),
        P("head", "req"),
        P("head"),
        P("req", None, "head"),
        P("req", None, "head"),
        P("req"),
    )
    return jax.shard_map(
        body_small if small else body_any,
        mesh=mesh,
        in_specs=placed,
        out_specs=(P("req", "head"), P("req", None, "head"), P("req", None, "head")),
        check_vma=False,
    )
```
